256 devices in a mesh: mode: 32 (over y, z_hi, core), tm: 8 (over z_lo, x).
Axes of the slice: x: 4, y: 4, z: 8 (z_hi: 4, z_lo: 2; z = z_hi * 2 + z_lo), core: 2. Of those that a mesh axis runs over, the one named last changes fastest.
Arguments:
- envelope: bfloat16 [512, 2, 32768], P('mode', None, 'tm'), may hold values from -6 to 6
- mode_profile: bfloat16 [512, 8192], replicated, may hold values from -0.375 to 0.375
- dispersion: float32 [3, 512], P(None, 'mode'), may hold values from -0.5 to 0.5
- kerr_gain: float32 [512], replicated, may hold values from 0.03 to 0.12
Outputs:
- advanced: float32 [512, 2, 32768], P('mode', None, 'tm')
The draws below stay inside these ranges and needn't reach their ends.
All inputs are finite; a program needn't handle non-finite values.
Results may differ from the reference program's by a relative error of at most 0.0027.
Values may be sent and summed in bfloat16 or wider, within the bound.
A program may use at most 64 MiB of HBM per device.

```python
import math
import jax
import jax.numpy as jnp
from jax import lax

MODES = 512
GRID = 8192
TIME = 32768


def block_levels(key, dims, shards, least, largest):
    level, own = 1.0, jax.random.fold_in(key, 6)
    for position, blocks in shards:
        steps = jnp.exp(jax.random.uniform(jax.random.fold_in(own, position), (blocks,), jnp.float32, least / len(shards), largest / len(shards)))
        level = level * jnp.repeat(steps, dims[position] // blocks).reshape([-1 if axis == position else 1 for axis in range(len(dims))])
    return level


def centred(key, dims, scale, reach, split=(), kind=jnp.bfloat16):
    loudness = block_levels(key, dims, split, -0.22, 0.18) if split else 1.0
    result = jax.random.normal(key, dims, jnp.float32) * scale * loudness
    return jnp.minimum(jnp.maximum(result, -reach), reach).astype(kind)


def setup_inputs(seed: int = 0) -> dict:
    seeds = jax.random.split(jax.random.key(seed), 5)
    envelope = centred(seeds[0], (MODES, 2, TIME), 1.0, 6.0, ((0, 32), (2, 8)))
    mode_profile = centred(seeds[1], (MODES, GRID), (MODES // 2) ** -0.5, 0.375)
    dispersion = jnp.clip(jax.random.uniform(seeds[2], (3, MODES), jnp.float32, -0.5, 0.5) * block_levels(seeds[2], (3, MODES), ((1, 32),), -0.4, 0.0), -0.5, 0.5)
    kerr_gain = jnp.clip(jnp.exp(jax.random.uniform(seeds[3], (MODES,), jnp.float32, math.log(0.03), math.log(0.12))), 0.03, 0.12)
    return dict(envelope=envelope, mode_profile=mode_profile, dispersion=dispersion, kerr_gain=kerr_gain)


FIRST_DIFF = (1.0 / 280, -4.0 / 105, 1.0 / 5, -4.0 / 5, 0.0, 4.0 / 5, -1.0 / 5, 4.0 / 105, -1.0 / 280)
SECOND_DIFF = (-1.0 / 560, 8.0 / 315, -1.0 / 5, 8.0 / 5, -205.0 / 72, 8.0 / 5, -1.0 / 5, 8.0 / 315, -1.0 / 560)
THIRD_DIFF = (7.0 / 240, -3.0 / 10, 169.0 / 120, -61.0 / 30, 0.0, 61.0 / 30, -169.0 / 120, 3.0 / 10, -7.0 / 240)


def stencil_terms(padded, dispersion, samples):
    walk_off = dispersion[0][:, None]
    spread = dispersion[1][:, None]
    skewed = dispersion[2][:, None]
    real_out = jnp.zeros((padded.shape[0], samples), jnp.float32)
    imag_out = jnp.zeros((padded.shape[0], samples), jnp.float32)
    for offset in range(9):
        shifted = lax.slice_in_dim(padded, offset, offset + samples, axis=2)
        direct = -walk_off * FIRST_DIFF[offset] + skewed * (THIRD_DIFF[offset] / 6.0)
        crossed = spread * (SECOND_DIFF[offset] / 2.0)
        real_out = real_out + direct * shifted[:, 0] + crossed * shifted[:, 1]
        imag_out = imag_out + direct * shifted[:, 1] - crossed * shifted[:, 0]
    return jnp.stack([real_out, imag_out], 1)


def kerr_terms(block, mode_profile, kerr_gain):
    mode_count = block.shape[0]
    columns = block.shape[2]
    half_modes = mode_count // 2
    grid_points = mode_profile.shape[1]
    grid_block = math.gcd(grid_points, 2048)
    stacked = block.reshape(mode_count, 2 * columns)
    field_pair = (stacked[:half_modes], stacked[half_modes:])

    def accumulate(running, block_index):
        profile_block = lax.dynamic_slice_in_dim(mode_profile, block_index * grid_block, grid_block, 1)
        profile_pair = (profile_block[:half_modes], profile_block[half_modes:])
        grid_fields = [lax.dot_general(profile_pair[which_pol], field_pair[which_pol], (((0,), (0,)), ((), ())), preferred_element_type=jnp.float32).reshape(grid_block, 2, columns) for which_pol in (0, 1)]
        intensity = grid_fields[0][:, 0] ** 2 + grid_fields[0][:, 1] ** 2 + grid_fields[1][:, 0] ** 2 + grid_fields[1][:, 1] ** 2
        cubic_pair = [(intensity[:, None, :] * grid_field).astype(jnp.bfloat16).reshape(grid_block, 2 * columns) for grid_field in grid_fields]
        projected = jnp.concatenate([jnp.dot(profile_pair[which_pol], cubic_pair[which_pol], preferred_element_type=jnp.float32) for which_pol in (0, 1)], 0)
        return running + projected, None

    running, unused = lax.scan(accumulate, jnp.zeros((mode_count, 2 * columns), jnp.float32), jnp.arange(grid_points // grid_block, dtype=jnp.int32))
    summed = running.reshape(mode_count, 2, columns)
    kerr_scale = (kerr_gain * (half_modes / grid_points))[:, None]
    return jnp.stack([-kerr_scale * summed[:, 1], kerr_scale * summed[:, 0]], 1)


def linear_rate(signal, dispersion):
    padded = jnp.concatenate([signal[:, :, -4:], signal, signal[:, :, :4]], 2)
    return stencil_terms(padded, dispersion, signal.shape[2])


def nonlinear_rate(signal, mode_profile, kerr_gain):
    mode_count = signal.shape[0]
    total_time = signal.shape[2]
    time_block = 512 if total_time % 512 == 0 else total_time
    blocks = signal.reshape(mode_count, 2, total_time // time_block, time_block).transpose(2, 0, 1, 3)

    def one_block(block):
        return kerr_terms(block, mode_profile, kerr_gain)

    results = lax.map(one_block, blocks)
    return results.transpose(1, 2, 0, 3).reshape(mode_count, 2, total_time)


def reference(envelope, mode_profile, dispersion, kerr_gain):
    initial = envelope.astype(jnp.float32)
    first_rate = linear_rate(initial, dispersion) + nonlinear_rate(envelope, mode_profile, kerr_gain)
    midway = (initial + first_rate).astype(jnp.bfloat16)
    second_rate = linear_rate(midway.astype(jnp.float32), dispersion) + nonlinear_rate(midway, mode_profile, kerr_gain)
    return initial + 0.5 * (first_rate + second_rate)
```

```python
import functools

import jax
import jax.numpy as jnp
import ml_dtypes
import numpy as np
from jax import lax
from jax.experimental import pallas as pl
from jax.experimental.pallas import tpu as pltpu
from jax.sharding import PartitionSpec as P

FIRST_DIFF = (1.0 / 280, -4.0 / 105, 1.0 / 5, -4.0 / 5, 0.0, 4.0 / 5, -1.0 / 5, 4.0 / 105, -1.0 / 280)
SECOND_DIFF = (-1.0 / 560, 8.0 / 315, -1.0 / 5, 8.0 / 5, -205.0 / 72, 8.0 / 5, -1.0 / 5, 8.0 / 315, -1.0 / 560)
THIRD_DIFF = (7.0 / 240, -3.0 / 10, 169.0 / 120, -61.0 / 30, 0.0, 61.0 / 30, -169.0 / 120, 3.0 / 10, -7.0 / 240)

MESH = pl.DeviceIdType.MESH
F32, BF16 = jnp.float32, jnp.bfloat16
NT = (((1,), (1,)), ((), ()))
TN = (((0,), (0,)), ((), ()))
W = 128


def hi_lo(x):
    hi = x.astype(ml_dtypes.bfloat16)
    lo = (x - hi.astype(np.float64)).astype(ml_dtypes.bfloat16)
    return hi, lo


def constants():
    taps = (np.array(FIRST_DIFF), np.array(SECOND_DIFF) / 2, np.array(THIRD_DIFF) / 6)
    main = np.zeros((W, 3 * W))
    halo = np.zeros((32, 6 * W))
    for which, tap in enumerate(taps):
        for t in range(W):
            for k in range(-4, 5):
                s, col = t + k, which * W + t
                if 0 <= s < W:
                    main[s, col] = tap[k + 4]
                else:
                    row = s + 4 if s < 0 else 16 + s - W
                    halo[row, col] = tap[k + 4]
                    halo[row + 4, 3 * W + col] = tap[k + 4]
    pick = np.zeros((32, 2 * W))
    for j in range(4):
        pick[j, j] = pick[4 + j, W + j] = 1
        pick[16 + j, W - 4 + j] = pick[20 + j, 2 * W - 4 + j] = 1
    return np.concatenate(hi_lo(main), 0), np.concatenate(hi_lo(halo), 0), pick.astype(ml_dtypes.bfloat16)


def dot(a, b, dims=(((1,), (0,)), ((), ()))):
    return lax.dot_general(a, b, dims, preferred_element_type=F32)


def kernel(
    peers, count, env_ref, prof_ref, disp_ref, gain_ref, main_ref, halo_ref, pick_ref, back_ref,
    env, prof, proft, field, mid, first, proj, sendbuf, incr, edges, halos, disp, drow, dall, coef,
    lsem, psem, ssem, rsem, dssem, drsem, hssem, hrsem, bssem, brsem,
):
    me, tm = lax.axis_index("mode"), lax.axis_index("tm")
    slabs = lax.axis_size("tm")
    grid = prof.shape[1]
    parts = psem.shape[0]
    width = grid // parts

    def to(peer):
        dy, dz, dc = peer
        y, z, c = me // 8, (me // 2) % 4, me % 2
        return ((y + dy) % 4) * 8 + ((z + dz) % 4) * 2 + (c + dc) % 2

    right = (lax.rem(me + 1, count), lax.rem(tm + (me + 1) // count, slabs))
    left = (lax.rem(me + count - 1, count), lax.rem(tm + slabs - (count - me) // count, slabs))

    barrier = pltpu.get_barrier_semaphore()
    for peer in peers:
        pl.semaphore_signal(barrier, inc=1, device_id=(to(peer), tm), device_id_type=MESH)
    for who in (left, right):
        pl.semaphore_signal(barrier, inc=1, device_id=who, device_id_type=MESH)

    env_in = pltpu.make_async_copy(env_ref, env, lsem.at[0])
    env_in.start()
    disp_in = pltpu.make_async_copy(disp_ref, disp, lsem.at[1])
    disp_in.start()

    def prof_in(i):
        cols = pl.ds(i * width, width)
        return pltpu.make_async_copy(prof_ref.at[:, cols], prof.at[:, cols], psem.at[i])

    for i in range(parts):
        prof_in(i).start()

    env_in.wait()
    for k in range(count):
        block = env[:, :, k * W : (k + 1) * W]
        sendbuf[k, :, 0:W] = block[:, 0, :]
        sendbuf[k, :, W : 2 * W] = block[:, 1, :]
    disp_in.wait()
    drow[...] = jnp.zeros_like(drow)
    drow[0:3, 0:16] = disp[...]
    rows = drow[...]
    packed = rows[0:1] + pltpu.roll(rows[1:2], 16, 1) + pltpu.roll(rows[2:3], 32, 1)
    dall[me] = packed

    pl.semaphore_wait(barrier, len(peers) + 2)

    my_rows = pl.ds(pl.multiple_of(me * 16, 16), 16)
    own = pltpu.make_async_copy(sendbuf.at[me], field.at[my_rows, :], lsem.at[2])
    own.start()
    sends, dsends = [], []
    for j, peer in enumerate(peers):
        sends.append(pltpu.make_async_remote_copy(
            src_ref=sendbuf.at[to(peer)], dst_ref=field.at[my_rows, :], send_sem=ssem.at[j], recv_sem=rsem.at[j],
            device_id=(to(peer), tm), device_id_type=MESH))
        sends[-1].start()
    for j, peer in enumerate(peers):
        dsends.append(pltpu.make_async_remote_copy(
            src_ref=dall.at[me], dst_ref=dall.at[me], send_sem=dssem.at[j], recv_sem=drsem.at[j],
            device_id=(to(peer), tm), device_id_type=MESH))
        dsends[-1].start()

    unit = (lax.broadcasted_iota(jnp.int32, (256, 256), 0) == lax.broadcasted_iota(jnp.int32, (256, 256), 1)).astype(BF16)
    for i in range(parts):
        prof_in(i).wait()

        def flip(b, _, i=i):
            at = pl.ds(pl.multiple_of(i * width + b * 256, 256), 256)
            for q in (0, 1):
                proft[at, 256 * q : 256 * q + 256] = dot(unit, prof[256 * q : 256 * q + 256, at], NT).astype(BF16)
            return 0

        lax.fori_loop(0, width // 256, flip, 0, unroll=True)

    diagonal = lax.broadcasted_iota(jnp.int32, (W, W), 0) == lax.broadcasted_iota(jnp.int32, (W, W), 1)
    for r in range(4):
        picked = jnp.where(diagonal, gain_ref[r : r + 1, :] * (256.0 / grid), 0.0)
        coef[3, r * W : (r + 1) * W, :] = jnp.broadcast_to(jnp.sum(picked, 1, keepdims=True), (W, W))

    own.wait()
    for cp in sends:
        cp.wait_send()
    for cp in sends:
        cp.wait_recv()

    def send_edges(values, turn):
        edges[turn] = dot(pick_ref[...], values, NT).astype(BF16).reshape(2, 16, 512)
        out = []
        for side, who in ((0, left), (1, right)):
            out.append(pltpu.make_async_remote_copy(
                src_ref=edges.at[turn, side], dst_ref=halos.at[turn, 1 - side], send_sem=hssem.at[turn, side],
                recv_sem=hrsem.at[turn, 1 - side], device_id=who, device_id_type=MESH))
            out[-1].start()
        return out

    hsends = send_edges(field[...], 0)
    for cp in dsends:
        cp.wait_send()
    for cp in dsends:
        cp.wait_recv()
    lane, sub = (lax.broadcasted_iota(jnp.int32, (16, W), d) for d in (1, 0))
    for i in range(count):
        row = jnp.broadcast_to(dall[i], (16, W))
        for d in range(3):
            column = jnp.sum(jnp.where(lane == sub + 16 * d, row, 0.0), 1, keepdims=True)
            coef[d, 16 * i : 16 * i + 16, :] = jnp.broadcast_to(column, (16, W))

    def kerr(src):
        step = 2048
        for b in range(grid // step):
            at = slice(b * step, (b + 1) * step)
            g = [dot(proft[at, 256 * q : 256 * q + 256], src[256 * q : 256 * q + 256, :]) for q in (0, 1)]
            level = g[0][:, :W] ** 2 + g[0][:, W:] ** 2 + g[1][:, :W] ** 2 + g[1][:, W:] ** 2
            level = jnp.concatenate([level, level], 1)
            for q in (0, 1):
                part = dot(prof[256 * q : 256 * q + 256, at], (level * g[q]).astype(BF16))
                if b == 0:
                    proj[256 * q : 256 * q + 256, :] = part
                else:
                    proj[256 * q : 256 * q + 256, :] += part

    def rate(src, turn):
        values = src[...]
        re, im = values[:, :W], values[:, W:]
        side = halos[turn].reshape(32, 512).astype(F32).T.astype(BF16)
        side = dot(jnp.concatenate([side, side], 1), halo_ref[...])
        d_re = dot(jnp.concatenate([re, re], 1), main_ref[...]) + side[:, : 3 * W]
        d_im = dot(jnp.concatenate([im, im], 1), main_ref[...]) + side[:, 3 * W :]
        walk, spread, skew, kerr_gain = coef[0], coef[1], coef[2], coef[3]
        out_re = skew * d_re[:, 2 * W :] - walk * d_re[:, :W] + spread * d_im[:, W : 2 * W] - kerr_gain * proj[:, W:]
        out_im = skew * d_im[:, 2 * W :] - walk * d_im[:, :W] - spread * d_re[:, W : 2 * W] + kerr_gain * proj[:, :W]
        return jnp.concatenate([out_re, out_im], 1)

    def wait_edges(copies):
        for cp in copies:
            cp.wait_send()
        for cp in copies:
            cp.wait_recv()

    kerr(field)
    wait_edges(hsends)
    first[...] = rate(field, 0)
    mid[...] = (field[...].astype(F32) + first[...]).astype(BF16)
    hsends = send_edges(mid[...], 1)
    kerr(mid)
    wait_edges(hsends)
    incr[...] = (0.5 * (first[...] + rate(mid, 1))).astype(BF16)

    own = pltpu.make_async_copy(incr.at[my_rows, :], back_ref.at[me], lsem.at[3])
    own.start()
    sends = []
    for j, peer in enumerate(peers):
        sends.append(pltpu.make_async_remote_copy(
            src_ref=incr.at[pl.ds(pl.multiple_of(to(peer) * 16, 16), 16), :], dst_ref=back_ref.at[me],
            send_sem=bssem.at[j], recv_sem=brsem.at[j], device_id=(to(peer), tm), device_id_type=MESH))
        sends[-1].start()
    own.wait()
    for cp in sends:
        cp.wait_send()
    for cp in sends:
        cp.wait_recv()


def on_device(envelope, mode_profile, dispersion, kerr_gain):
    count = lax.axis_size("mode")
    peers = [(dy, dz, dc) for dy in range(4) for dz in range(4) for dc in range(2) if (dy, dz, dc) != (0, 0, 0)]
    peers.sort(key=lambda d: -(min(d[0], 4 - d[0]) + 2 * min(d[1], 4 - d[1])))
    n = len(peers)
    modes, grid = mode_profile.shape
    main, halo, pick = (jnp.asarray(c) for c in constants())
    hbm, vmem = pl.BlockSpec(memory_space=pl.ANY), pl.BlockSpec(memory_space=pltpu.VMEM)
    dma = pltpu.SemaphoreType.DMA
    back = pl.pallas_call(
        functools.partial(kernel, peers, count),
        out_shape=jax.ShapeDtypeStruct((count, 16, 2 * W), BF16),
        in_specs=[hbm, hbm, hbm, vmem, vmem, vmem, vmem],
        out_specs=hbm,
        scratch_shapes=[
            pltpu.VMEM(envelope.shape, BF16),
            pltpu.VMEM((modes, grid), BF16),
            pltpu.VMEM((grid, modes), BF16),
            pltpu.VMEM((modes, 2 * W), BF16),
            pltpu.VMEM((modes, 2 * W), BF16),
            pltpu.VMEM((modes, 2 * W), F32),
            pltpu.VMEM((modes, 2 * W), F32),
            pltpu.VMEM((count, 16, 2 * W), BF16),
            pltpu.VMEM((modes, 2 * W), BF16),
            pltpu.VMEM((2, 2, 16, modes), BF16),
            pltpu.VMEM((2, 2, 16, modes), BF16),
            pltpu.VMEM((3, 16), F32),
            pltpu.VMEM((8, W), F32),
            pltpu.VMEM((count, 1, W), F32),
            pltpu.VMEM((4, modes, W), F32),
            dma((4,)), dma((4,)), dma((n,)), dma((n,)), dma((n,)), dma((n,)),
            dma((2, 2)), dma((2, 2)), dma((n,)), dma((n,)),
        ],
        compiler_params=pltpu.CompilerParams(collective_id=1, has_side_effects=True, vmem_limit_bytes=60 * 2**20),
    )(envelope, mode_profile, dispersion, kerr_gain.reshape(4, W), main, halo, pick)
    added = back.reshape(count, 16, 2, W).transpose(1, 2, 0, 3).reshape(envelope.shape)
    return envelope.astype(F32) + added.astype(F32)


def solution(mesh):
    placed = (P("mode", None, "tm"), P(), P(None, "mode"), P())
    return jax.shard_map(
        on_device, mesh=mesh, in_specs=placed, out_specs=P("mode", None, "tm"), check_vma=False
    )
```

```python
import functools

import jax
import jax.numpy as jnp
import ml_dtypes
import numpy as np
from jax import lax
from jax.experimental import pallas as pl
from jax.experimental.pallas import tpu as pltpu
from jax.sharding import PartitionSpec as P

FIRST_DIFF = (1.0 / 280, -4.0 / 105, 1.0 / 5, -4.0 / 5, 0.0, 4.0 / 5, -1.0 / 5, 4.0 / 105, -1.0 / 280)
SECOND_DIFF = (-1.0 / 560, 8.0 / 315, -1.0 / 5, 8.0 / 5, -205.0 / 72, 8.0 / 5, -1.0 / 5, 8.0 / 315, -1.0 / 560)
THIRD_DIFF = (7.0 / 240, -3.0 / 10, 169.0 / 120, -61.0 / 30, 0.0, 61.0 / 30, -169.0 / 120, 3.0 / 10, -7.0 / 240)

MESH = pl.DeviceIdType.MESH
F32, BF16 = jnp.float32, jnp.bfloat16
NT = (((1,), (1,)), ((), ()))
TN = (((0,), (0,)), ((), ()))
W = 128


def hi_lo(x):
    hi = x.astype(ml_dtypes.bfloat16)
    lo = (x - hi.astype(np.float64)).astype(ml_dtypes.bfloat16)
    return hi, lo


def constants():
    taps = (np.array(FIRST_DIFF), np.array(SECOND_DIFF) / 2, np.array(THIRD_DIFF) / 6)
    main = np.zeros((W, 3 * W))
    halo = np.zeros((32, 6 * W))
    for which, tap in enumerate(taps):
        for t in range(W):
            for k in range(-4, 5):
                s, col = t + k, which * W + t
                if 0 <= s < W:
                    main[s, col] = tap[k + 4]
                else:
                    row = s + 4 if s < 0 else 16 + s - W
                    halo[row, col] = tap[k + 4]
                    halo[row + 4, 3 * W + col] = tap[k + 4]
    pick = np.zeros((32, 2 * W))
    for j in range(4):
        pick[j, j] = pick[4 + j, W + j] = 1
        pick[16 + j, W - 4 + j] = pick[20 + j, 2 * W - 4 + j] = 1
    return np.concatenate(hi_lo(main), 0), np.concatenate(hi_lo(halo), 0), pick.astype(ml_dtypes.bfloat16)


def dot(a, b, dims=(((1,), (0,)), ((), ()))):
    return lax.dot_general(a, b, dims, preferred_element_type=F32)


def place(y, z, c):
    z = z + (y % 2) * (3 - 2 * z)
    return y * 8 + z * 2 + (c + z) % 2


def device_at(pos):
    y, z = pos // 8, (pos // 2) % 4
    c = (pos % 2 + z) % 2
    z = z + (y % 2) * (3 - 2 * z)
    return y * 8 + z * 2 + c


def kernel(
    peers, count, env_ref, prof_ref, disp_ref, gain_ref, main_ref, halo_ref, pick_ref, back_ref,
    env, prof, proft, own_grid, cubic, field, mid, first, proj, sendbuf, incr, edges, halos, disp, drow, dall, coef, got,
    gain, main, halo, pick, lsem, psem, ssem, rsem, dssem, drsem, hssem, hrsem, bssem, brsem,
):
    me, tm = lax.axis_index("mode"), lax.axis_index("tm")
    slabs = lax.axis_size("tm")
    grid = prof.shape[1]
    parts = psem.shape[1]
    width = grid // parts
    y, z, c = me // 8, (me // 2) % 4, me % 2
    half = y // 2

    def to(peer):
        dy, dz, dc = peer
        py = (y, y + 1 - 2 * (y % 2), (y + 2) % 4, 3 - y)[dy]
        return py * 8 + ((z + dz) % 4) * 2 + (c + dc) % 2

    def back_from(peer):
        return to((peer[0], (4 - peer[1]) % 4, peer[2]))

    def rows(device, pol):
        return pl.ds(pl.multiple_of(((device + 16 * pol) % count) * 16, 16), 16)

    here = place(y, z, c)
    right = (device_at((here + 1) % count), (tm + (here + 1) // count) % slabs)
    left = (device_at((here + count - 1) % count), (tm + slabs - (count - here) // count) % slabs)

    barrier = pltpu.get_barrier_semaphore()
    for peer in peers:
        pl.semaphore_signal(barrier, inc=1, device_id=(to(peer), tm), device_id_type=MESH)
    for who in (left, right):
        pl.semaphore_signal(barrier, inc=1, device_id=who, device_id_type=MESH)

    loads = [
        pltpu.make_async_copy(a, b, lsem.at[i])
        for i, (a, b) in enumerate(
            ((env_ref, env), (disp_ref, disp), (gain_ref, gain), (pick_ref, pick), (main_ref, main), (halo_ref, halo))
        )
    ]
    for cp in loads:
        cp.start()

    def prof_in(i, q):
        cols = pl.ds(i * width, width)
        pol = pl.ds(pl.multiple_of(256 * ((half + q) % 2), 256), 256)
        return pltpu.make_async_copy(prof_ref.at[pol, cols], prof.at[256 * q : 256 * q + 256, cols], psem.at[q, i])

    for i in range(parts):
        for q in (0, 1):
            prof_in(i, q).start()

    loads[0].wait()
    for p in range(count):
        k = place(p // 8, (p // 2) % 4, p % 2)
        block = env[:, :, k * W : (k + 1) * W]
        sendbuf[p, :, 0:W] = block[:, 0, :]
        sendbuf[p, :, W : 2 * W] = block[:, 1, :]
    loads[1].wait()
    drow[...] = jnp.zeros_like(drow)
    drow[0:3, 0:16] = disp[...]
    lines = drow[...]
    drow[0:1, :] = lines[0:1] + pltpu.roll(lines[1:2], 16, 1) + pltpu.roll(lines[2:3], 32, 1)
    dall[me % 16] = drow[0:1, :]

    pl.semaphore_wait(barrier, len(peers) + 2)

    own = pltpu.make_async_copy(sendbuf.at[me], field.at[rows(me, half), :], lsem.at[6])
    own.start()
    sends, dsends = [], []
    for j, peer in enumerate(peers):
        other = to(peer)
        sends.append(pltpu.make_async_remote_copy(
            src_ref=sendbuf.at[other], dst_ref=field.at[rows(me, half if peer[0] < 2 else 1 - half), :],
            send_sem=ssem.at[j], recv_sem=rsem.at[j], device_id=(other, tm), device_id_type=MESH))
        sends[-1].start()

    unit = (lax.broadcasted_iota(jnp.int32, (256, 256), 0) == lax.broadcasted_iota(jnp.int32, (256, 256), 1)).astype(BF16)
    for i in range(parts):
        for q in (0, 1):
            prof_in(i, q).wait()

        def flip(b, _, i=i):
            at = pl.ds(pl.multiple_of(i * width + b * 256, 256), 256)
            for q in (0, 1):
                proft[at, 256 * q : 256 * q + 256] = dot(unit, prof[256 * q : 256 * q + 256, at], NT).astype(BF16)
            return 0

        lax.fori_loop(0, width // 256, flip, 0, unroll=True)

    for j, peer in enumerate(peers):
        slot = (me + 16 * (half if peer[0] < 2 else 1 - half)) % count
        dsends.append(pltpu.make_async_remote_copy(
            src_ref=drow.at[0:1], dst_ref=dall.at[slot], send_sem=dssem.at[j], recv_sem=drsem.at[j],
            device_id=(to(peer), tm), device_id_type=MESH))
        dsends[-1].start()

    loads[2].wait()
    diagonal = lax.broadcasted_iota(jnp.int32, (W, W), 0) == lax.broadcasted_iota(jnp.int32, (W, W), 1)
    for r in range(4):
        picked = jnp.where(diagonal, gain[pl.ds((r + 2 * half) % 4, 1), :] * (256.0 / grid), 0.0)
        coef[3, r * W : (r + 1) * W, :] = jnp.broadcast_to(jnp.sum(picked, 1, keepdims=True), (W, W))

    for cp in loads[3:]:
        cp.wait()

    def grid_field(src, q, at):
        return dot(proft[at, 256 * q : 256 * q + 256], src[256 * q : 256 * q + 256, :])

    step = 2048
    blocks = [slice(b * step, (b + 1) * step) for b in range(grid // step)]

    own.wait()
    for cp, peer in zip(sends, peers):
        if peer[0] < 2:
            cp.wait_recv()
    for at in blocks:
        own_grid[at, :] = grid_field(field, 0, at)
    for cp, peer in zip(sends, peers):
        if peer[0] >= 2:
            cp.wait_recv()

    def send_edges(values, turn):
        edges[turn] = dot(pick[...], values, NT).astype(BF16).reshape(2, 16, 512)
        out = []
        for side, who in ((0, left), (1, right)):
            out.append(pltpu.make_async_remote_copy(
                src_ref=edges.at[turn, side], dst_ref=halos.at[turn, 1 - side], send_sem=hssem.at[turn, side],
                recv_sem=hrsem.at[turn, 1 - side], device_id=who, device_id_type=MESH))
            out[-1].start()
        return out

    hsends = send_edges(field[...], 0)
    for cp in dsends:
        cp.wait_recv()
    lane, sub = (lax.broadcasted_iota(jnp.int32, (16, W), d) for d in (1, 0))
    for i in range(count):
        row = jnp.broadcast_to(dall[i], (16, W))
        for d in range(3):
            column = jnp.sum(jnp.where(lane == sub + 16 * d, row, 0.0), 1, keepdims=True)
            coef[d, 16 * i : 16 * i + 16, :] = jnp.broadcast_to(column, (16, W))

    def cube(g):
        level = g[0][:, :W] ** 2 + g[0][:, W:] ** 2 + g[1][:, :W] ** 2 + g[1][:, W:] ** 2
        level = jnp.concatenate([level, level], 1)
        return [(level * part).astype(BF16) for part in g]

    def linear(src, turn, q):
        at = slice(256 * q, 256 * q + 256)
        values = src[at, :]
        re, im = values[:, :W], values[:, W:]
        ends = [
            halos[turn, s, :, pl.ds(pl.multiple_of(256 * ((q + half + who[0] // 16) % 2), 256), 256)]
            for s, who in ((0, left), (1, right))
        ]
        side = jnp.concatenate(ends, 0).astype(F32).T.astype(BF16)
        side = dot(jnp.concatenate([side, side], 1), halo[...])
        d_re = dot(jnp.concatenate([re, re], 1), main[...]) + side[:, : 3 * W]
        d_im = dot(jnp.concatenate([im, im], 1), main[...]) + side[:, 3 * W :]
        walk, spread, skew = (coef[d, at, :] for d in range(3))
        out_re = skew * d_re[:, 2 * W :] - walk * d_re[:, :W] + spread * d_im[:, W : 2 * W]
        out_im = skew * d_im[:, 2 * W :] - walk * d_im[:, :W] - spread * d_re[:, W : 2 * W]
        return jnp.concatenate([out_re, out_im], 1)

    def turned(values, q):
        scale = coef[3, 256 * q : 256 * q + 256, :]
        return jnp.concatenate([-scale * values[:, W:], scale * values[:, :W]], 1)

    for b, at in enumerate(blocks):
        parts_ = cube([own_grid[at, :], grid_field(field, 1, at)])
        for q in (0, 1):
            part = dot(prof[256 * q : 256 * q + 256, at], parts_[q])
            if b == 0:
                proj[256 * q : 256 * q + 256, :] = part
            else:
                proj[256 * q : 256 * q + 256, :] += part
    for cp in hsends:
        cp.wait_recv()
    for q in (0, 1):
        at = slice(256 * q, 256 * q + 256)
        rate = linear(field, 0, q) + turned(proj[at, :], q)
        first[at, :] = rate
        mid[at, :] = (field[at, :].astype(F32) + rate).astype(BF16)
    hsends += send_edges(mid[...], 1)

    for at in blocks:
        parts_ = cube([grid_field(mid, q, at) for q in (0, 1)])
        for q in (0, 1):
            cubic[q, at, :] = parts_[q]
    for cp in hsends[2:]:
        cp.wait_recv()
    returns = {}
    for q in (1, 0):
        at = slice(256 * q, 256 * q + 256)
        known = first[at, :] + linear(mid, 1, q)
        proj[at, :] = dot(prof[at, :], cubic[q])
        incr[at, :] = (0.5 * (known + turned(proj[at, :], q))).astype(BF16)
        for j, peer in enumerate(peers):
            if (peer[0] >= 2) == (q == 1):
                other = to(peer)
                returns[j] = pltpu.make_async_remote_copy(
                    src_ref=incr.at[rows(other, half), :], dst_ref=got.at[me], send_sem=bssem.at[j],
                    recv_sem=brsem.at[j], device_id=(other, tm), device_id_type=MESH)
                returns[j].start()
    own = pltpu.make_async_copy(incr.at[rows(me, half), :], got.at[me], lsem.at[7])
    own.start()

    def hand_on(source):
        k = place(source // 8, (source // 2) % 4, source % 2)
        values = got[source].astype(F32)
        pair = jnp.stack([values[:, :W], values[:, W:]], 1).astype(BF16)
        back_ref[:, :, pl.ds(pl.multiple_of(k * W, W), W)] = pair

    own.wait()
    hand_on(me)
    for near in range(n_far(peers)):
        for j, peer in enumerate(peers):
            if distance(peer) == near:
                returns[j].wait_recv()
                hand_on(back_from(peer))
    for cp in [*sends, *dsends, *hsends, *returns.values()]:
        cp.wait_send()


def distance(peer):
    dy, dz, dc = peer
    return min(dz, 4 - dz) + 4 * (dy // 2)


def n_far(peers):
    return 1 + max(distance(p) for p in peers)


def on_device(envelope, mode_profile, dispersion, kerr_gain):
    count = lax.axis_size("mode")
    peers = [(dy, dz, dc) for dy in range(4) for dz in (2, 1, 3, 0) for dc in range(2) if (dy, dz, dc) != (0, 0, 0)]
    peers.sort(key=lambda d: (d[0] // 2, -min(d[1], 4 - d[1])))
    n = len(peers)
    modes, grid = mode_profile.shape
    consts = [jnp.asarray(c) for c in constants()]
    hbm, vmem = pl.BlockSpec(memory_space=pl.ANY), pl.BlockSpec(memory_space=pltpu.VMEM)
    dma = pltpu.SemaphoreType.DMA
    added = pl.pallas_call(
        functools.partial(kernel, peers, count),
        out_shape=jax.ShapeDtypeStruct(envelope.shape, BF16),
        in_specs=[hbm] * 7,
        out_specs=vmem,
        scratch_shapes=[
            pltpu.VMEM(envelope.shape, BF16),
            pltpu.VMEM((modes, grid), BF16),
            pltpu.VMEM((grid, modes), BF16),
            pltpu.VMEM((grid, 2 * W), F32),
            pltpu.VMEM((2, grid, 2 * W), BF16),
            pltpu.VMEM((modes, 2 * W), BF16),
            pltpu.VMEM((modes, 2 * W), BF16),
            pltpu.VMEM((modes, 2 * W), F32),
            pltpu.VMEM((modes, 2 * W), F32),
            pltpu.VMEM((count, 16, 2 * W), BF16),
            pltpu.VMEM((modes, 2 * W), BF16),
            pltpu.VMEM((2, 2, 16, modes), BF16),
            pltpu.VMEM((2, 2, 16, modes), BF16),
            pltpu.VMEM((3, 16), F32),
            pltpu.VMEM((8, W), F32),
            pltpu.VMEM((count, 1, W), F32),
            pltpu.VMEM((4, modes, W), F32),
            pltpu.VMEM((count, 16, 2 * W), BF16),
            pltpu.VMEM((4, W), F32),
            *[pltpu.VMEM(c.shape, BF16) for c in consts],
            dma((8,)), dma((2, 4)), dma((n,)), dma((n,)), dma((n,)), dma((n,)),
            dma((2, 2)), dma((2, 2)), dma((n,)), dma((n,)),
        ],
        compiler_params=pltpu.CompilerParams(collective_id=1, has_side_effects=True, vmem_limit_bytes=60 * 2**20),
    )(envelope, mode_profile, dispersion, kerr_gain.reshape(4, W), *consts)
    return envelope.astype(F32) + added.astype(F32)


def solution(mesh):
    placed = (P("mode", None, "tm"), P(), P(None, "mode"), P())
    return jax.shard_map(
        on_device, mesh=mesh, in_specs=placed, out_specs=P("mode", None, "tm"), check_vma=False
    )
```

```python
import functools

import jax
import jax.numpy as jnp
import ml_dtypes
import numpy as np
from jax import lax
from jax.experimental import pallas as pl
from jax.experimental.pallas import tpu as pltpu
from jax.sharding import PartitionSpec as P

FIRST_DIFF = (1.0 / 280, -4.0 / 105, 1.0 / 5, -4.0 / 5, 0.0, 4.0 / 5, -1.0 / 5, 4.0 / 105, -1.0 / 280)
SECOND_DIFF = (-1.0 / 560, 8.0 / 315, -1.0 / 5, 8.0 / 5, -205.0 / 72, 8.0 / 5, -1.0 / 5, 8.0 / 315, -1.0 / 560)
THIRD_DIFF = (7.0 / 240, -3.0 / 10, 169.0 / 120, -61.0 / 30, 0.0, 61.0 / 30, -169.0 / 120, 3.0 / 10, -7.0 / 240)

MESH = pl.DeviceIdType.MESH
F32, BF16 = jnp.float32, jnp.bfloat16
NT = (((1,), (1,)), ((), ()))
TN = (((0,), (0,)), ((), ()))
W = 128


def hi_lo(x):
    hi = x.astype(ml_dtypes.bfloat16)
    lo = (x - hi.astype(np.float64)).astype(ml_dtypes.bfloat16)
    return hi, lo


def constants():
    taps = (np.array(FIRST_DIFF), np.array(SECOND_DIFF) / 2, np.array(THIRD_DIFF) / 6)
    main = np.zeros((W, 3 * W))
    halo = np.zeros((32, 6 * W))
    for which, tap in enumerate(taps):
        for t in range(W):
            for k in range(-4, 5):
                s, col = t + k, which * W + t
                if 0 <= s < W:
                    main[s, col] = tap[k + 4]
                else:
                    row = s + 4 if s < 0 else 16 + s - W
                    halo[row, col] = tap[k + 4]
                    halo[row + 4, 3 * W + col] = tap[k + 4]
    pick = np.zeros((32, 2 * W))
    for j in range(4):
        pick[j, j] = pick[4 + j, W + j] = 1
        pick[16 + j, W - 4 + j] = pick[20 + j, 2 * W - 4 + j] = 1
    return np.concatenate(hi_lo(main), 0), np.concatenate(hi_lo(halo), 0), pick.astype(ml_dtypes.bfloat16)


def dot(a, b, dims=(((1,), (0,)), ((), ()))):
    return lax.dot_general(a, b, dims, preferred_element_type=F32)


def place(y, z, c):
    z = z + (y % 2) * (3 - 2 * z)
    return y * 8 + z * 2 + (c + z) % 2


def device_at(pos):
    y, z = pos // 8, (pos // 2) % 4
    c = (pos % 2 + z) % 2
    z = z + (y % 2) * (3 - 2 * z)
    return y * 8 + z * 2 + c


def kernel(
    peers, count, env_ref, prof_ref, disp_ref, gain_ref, main_ref, halo_ref, pick_ref, out_ref,
    env, prof, proft, own_grid, cubic, field, mid, first, proj, sendbuf, incr, edges, halos, disp, drow, dall, coef, got,
    gain, main, halo, pick, lsem, psem, ssem, rsem, dssem, drsem, hssem, hrsem, bssem, brsem,
):
    me, tm = lax.axis_index("mode"), lax.axis_index("tm")
    slabs = lax.axis_size("tm")
    grid = prof.shape[1]
    parts = psem.shape[1]
    width = grid // parts
    y, z, c = me // 8, (me // 2) % 4, me % 2
    half = y // 2

    def to(peer):
        dy, dz, dc = peer
        py = (y, y + 1 - 2 * (y % 2), (y + 2) % 4, 3 - y)[dy]
        return py * 8 + ((z + dz) % 4) * 2 + (c + dc) % 2

    def back_from(peer):
        return to((peer[0], (4 - peer[1]) % 4, peer[2]))

    def rows(device, pol):
        return pl.ds(pl.multiple_of(((device + 16 * pol) % count) * 16, 16), 16)

    here = place(y, z, c)
    right = (device_at((here + 1) % count), (tm + (here + 1) // count) % slabs)
    left = (device_at((here + count - 1) % count), (tm + slabs - (count - here) // count) % slabs)

    barrier = pltpu.get_barrier_semaphore()
    for peer in peers:
        pl.semaphore_signal(barrier, inc=1, device_id=(to(peer), tm), device_id_type=MESH)
    for who in (left, right):
        pl.semaphore_signal(barrier, inc=1, device_id=who, device_id_type=MESH)

    loads = [
        pltpu.make_async_copy(a, b, lsem.at[i])
        for i, (a, b) in enumerate(
            ((env_ref, env), (disp_ref, disp), (gain_ref, gain), (pick_ref, pick), (main_ref, main), (halo_ref, halo))
        )
    ]
    for cp in loads:
        cp.start()

    def prof_in(i, q):
        cols = pl.ds(i * width, width)
        pol = pl.ds(pl.multiple_of(256 * ((half + q) % 2), 256), 256)
        return pltpu.make_async_copy(prof_ref.at[pol, cols], prof.at[256 * q : 256 * q + 256, cols], psem.at[q, i])

    for i in range(parts):
        for q in (0, 1):
            prof_in(i, q).start()

    loads[0].wait()
    for p in range(count):
        k = place(p // 8, (p // 2) % 4, p % 2)
        block = env[:, :, k * W : (k + 1) * W]
        sendbuf[p, :, 0:W] = block[:, 0, :]
        sendbuf[p, :, W : 2 * W] = block[:, 1, :]
    loads[1].wait()
    drow[...] = jnp.zeros_like(drow)
    drow[0:3, 0:16] = disp[...]
    lines = drow[...]
    drow[0:1, :] = lines[0:1] + pltpu.roll(lines[1:2], 16, 1) + pltpu.roll(lines[2:3], 32, 1)
    dall[me % 16] = drow[0:1, :]

    pl.semaphore_wait(barrier, len(peers) + 2)

    own = pltpu.make_async_copy(sendbuf.at[me], field.at[rows(me, half), :], lsem.at[6])
    own.start()
    sends, dsends = [], []
    for j, peer in enumerate(peers):
        other = to(peer)
        sends.append(pltpu.make_async_remote_copy(
            src_ref=sendbuf.at[other], dst_ref=field.at[rows(me, half if peer[0] < 2 else 1 - half), :],
            send_sem=ssem.at[j], recv_sem=rsem.at[j], device_id=(other, tm), device_id_type=MESH))
        sends[-1].start()

    unit = (lax.broadcasted_iota(jnp.int32, (256, 256), 0) == lax.broadcasted_iota(jnp.int32, (256, 256), 1)).astype(BF16)
    for i in range(parts):
        for q in (0, 1):
            prof_in(i, q).wait()

        def flip(b, _, i=i):
            at = pl.ds(pl.multiple_of(i * width + b * 256, 256), 256)
            for q in (0, 1):
                proft[at, 256 * q : 256 * q + 256] = dot(unit, prof[256 * q : 256 * q + 256, at], NT).astype(BF16)
            return 0

        lax.fori_loop(0, width // 256, flip, 0, unroll=True)

    for j, peer in enumerate(peers):
        slot = (me + 16 * (half if peer[0] < 2 else 1 - half)) % count
        dsends.append(pltpu.make_async_remote_copy(
            src_ref=drow.at[0:1], dst_ref=dall.at[slot], send_sem=dssem.at[j], recv_sem=drsem.at[j],
            device_id=(to(peer), tm), device_id_type=MESH))
        dsends[-1].start()

    loads[2].wait()
    diagonal = lax.broadcasted_iota(jnp.int32, (W, W), 0) == lax.broadcasted_iota(jnp.int32, (W, W), 1)
    for r in range(4):
        picked = jnp.where(diagonal, gain[pl.ds((r + 2 * half) % 4, 1), :] * (256.0 / grid), 0.0)
        coef[3, r * W : (r + 1) * W, :] = jnp.broadcast_to(jnp.sum(picked, 1, keepdims=True), (W, W))

    for cp in loads[3:]:
        cp.wait()

    def grid_field(src, q, at):
        return dot(proft[at, 256 * q : 256 * q + 256], src[256 * q : 256 * q + 256, :])

    step = 2048
    blocks = [slice(b * step, (b + 1) * step) for b in range(grid // step)]

    own.wait()
    for cp, peer in zip(sends, peers):
        if peer[0] < 2:
            cp.wait_recv()
    for at in blocks:
        own_grid[at, :] = grid_field(field, 0, at)
    for cp, peer in zip(sends, peers):
        if peer[0] >= 2:
            cp.wait_recv()

    def send_edges(values, turn):
        edges[turn] = dot(pick[...], values, NT).astype(BF16).reshape(2, 16, 512)
        out = []
        for side, who in ((0, left), (1, right)):
            out.append(pltpu.make_async_remote_copy(
                src_ref=edges.at[turn, side], dst_ref=halos.at[turn, 1 - side], send_sem=hssem.at[turn, side],
                recv_sem=hrsem.at[turn, 1 - side], device_id=who, device_id_type=MESH))
            out[-1].start()
        return out

    hsends = send_edges(field[...], 0)
    for cp in dsends:
        cp.wait_recv()
    lane, sub = (lax.broadcasted_iota(jnp.int32, (16, W), d) for d in (1, 0))
    for i in range(count):
        row = jnp.broadcast_to(dall[i], (16, W))
        for d in range(3):
            column = jnp.sum(jnp.where(lane == sub + 16 * d, row, 0.0), 1, keepdims=True)
            coef[d, 16 * i : 16 * i + 16, :] = jnp.broadcast_to(column, (16, W))

    def cube(g):
        level = g[0][:, :W] ** 2 + g[0][:, W:] ** 2 + g[1][:, :W] ** 2 + g[1][:, W:] ** 2
        level = jnp.concatenate([level, level], 1)
        return [(level * part).astype(BF16) for part in g]

    def interior(src, q):
        at = slice(256 * q, 256 * q + 256)
        values = src[at, :]
        re, im = values[:, :W], values[:, W:]
        d_re = dot(jnp.concatenate([re, re], 1), main[...])
        d_im = dot(jnp.concatenate([im, im], 1), main[...])
        return combined(d_re, d_im, at)

    def fringe(turn, q):
        ends = [
            halos[turn, s, :, pl.ds(pl.multiple_of(256 * ((q + half + who[0] // 16) % 2), 256), 256)]
            for s, who in ((0, left), (1, right))
        ]
        side = jnp.concatenate(ends, 0).astype(F32).T.astype(BF16)
        side = dot(jnp.concatenate([side, side], 1), halo[...])
        return combined(side[:, : 3 * W], side[:, 3 * W :], slice(256 * q, 256 * q + 256))

    def combined(d_re, d_im, at):
        walk, spread, skew = (coef[d, at, :] for d in range(3))
        out_re = skew * d_re[:, 2 * W :] - walk * d_re[:, :W] + spread * d_im[:, W : 2 * W]
        out_im = skew * d_im[:, 2 * W :] - walk * d_im[:, :W] - spread * d_re[:, W : 2 * W]
        return jnp.concatenate([out_re, out_im], 1)

    def turned(values, q):
        scale = coef[3, 256 * q : 256 * q + 256, :]
        return jnp.concatenate([-scale * values[:, W:], scale * values[:, :W]], 1)

    for q in (0, 1):
        first[256 * q : 256 * q + 256, :] = interior(field, q)
    for b, at in enumerate(blocks):
        parts_ = cube([own_grid[at, :], grid_field(field, 1, at)])
        for q in (0, 1):
            part = dot(prof[256 * q : 256 * q + 256, at], parts_[q])
            if b == 0:
                proj[256 * q : 256 * q + 256, :] = part
            else:
                proj[256 * q : 256 * q + 256, :] += part
    for cp in hsends:
        cp.wait_recv()
    for q in (0, 1):
        at = slice(256 * q, 256 * q + 256)
        rate = first[at, :] + fringe(0, q) + turned(proj[at, :], q)
        first[at, :] = rate
        mid[at, :] = (field[at, :].astype(F32) + rate).astype(BF16)
    hsends += send_edges(mid[...], 1)

    for q in (0, 1):
        first[256 * q : 256 * q + 256, :] += interior(mid, q)
    for at in blocks:
        parts_ = cube([grid_field(mid, q, at) for q in (0, 1)])
        for q in (0, 1):
            cubic[q, at, :] = parts_[q]
    returns = {}
    for q in (1, 0):
        at = slice(256 * q, 256 * q + 256)
        proj[at, :] = dot(prof[at, :], cubic[q])
        if q == 1:
            for cp in hsends[2:]:
                cp.wait_recv()
        incr[at, :] = (0.5 * (first[at, :] + fringe(1, q) + turned(proj[at, :], q))).astype(BF16)
        for j, peer in enumerate(peers):
            if (peer[0] >= 2) == (q == 1):
                other = to(peer)
                returns[j] = pltpu.make_async_remote_copy(
                    src_ref=incr.at[rows(other, half), :], dst_ref=got.at[me], send_sem=bssem.at[j],
                    recv_sem=brsem.at[j], device_id=(other, tm), device_id_type=MESH)
                returns[j].start()
    own = pltpu.make_async_copy(incr.at[rows(me, half), :], got.at[me], lsem.at[7])
    own.start()

    def hand_on(source):
        k = place(source // 8, (source // 2) % 4, source % 2)
        values = got[source].astype(F32)
        pair = jnp.stack([values[:, :W], values[:, W:]], 1)
        at = pl.ds(pl.multiple_of(k * W, W), W)
        out_ref[:, :, at] = env[:, :, at].astype(F32) + pair

    own.wait()
    hand_on(me)
    for near in range(n_far(peers)):
        for j, peer in enumerate(peers):
            if distance(peer) == near:
                returns[j].wait_recv()
                hand_on(back_from(peer))
    for cp in [*sends, *dsends, *hsends, *returns.values()]:
        cp.wait_send()


def distance(peer):
    dy, dz, dc = peer
    return min(dz, 4 - dz) + 4 * (dy // 2)


def n_far(peers):
    return 1 + max(distance(p) for p in peers)


def on_device(envelope, mode_profile, dispersion, kerr_gain):
    count = lax.axis_size("mode")
    peers = [(dy, dz, dc) for dy in range(4) for dz in (2, 1, 3, 0) for dc in range(2) if (dy, dz, dc) != (0, 0, 0)]
    peers.sort(key=lambda d: (d[0] // 2, -min(d[1], 4 - d[1])))
    n = len(peers)
    modes, grid = mode_profile.shape
    consts = [jnp.asarray(c) for c in constants()]
    hbm, vmem = pl.BlockSpec(memory_space=pl.ANY), pl.BlockSpec(memory_space=pltpu.VMEM)
    dma = pltpu.SemaphoreType.DMA
    return pl.pallas_call(
        functools.partial(kernel, peers, count),
        out_shape=pltpu.VMEM(envelope.shape, F32),
        in_specs=[hbm] * 7,
        out_specs=vmem,
        scratch_shapes=[
            pltpu.VMEM(envelope.shape, BF16),
            pltpu.VMEM((modes, grid), BF16),
            pltpu.VMEM((grid, modes), BF16),
            pltpu.VMEM((grid, 2 * W), F32),
            pltpu.VMEM((2, grid, 2 * W), BF16),
            pltpu.VMEM((modes, 2 * W), BF16),
            pltpu.VMEM((modes, 2 * W), BF16),
            pltpu.VMEM((modes, 2 * W), F32),
            pltpu.VMEM((modes, 2 * W), F32),
            pltpu.VMEM((count, 16, 2 * W), BF16),
            pltpu.VMEM((modes, 2 * W), BF16),
            pltpu.VMEM((2, 2, 16, modes), BF16),
            pltpu.VMEM((2, 2, 16, modes), BF16),
            pltpu.VMEM((3, 16), F32),
            pltpu.VMEM((8, W), F32),
            pltpu.VMEM((count, 1, W), F32),
            pltpu.VMEM((4, modes, W), F32),
            pltpu.VMEM((count, 16, 2 * W), BF16),
            pltpu.VMEM((4, W), F32),
            *[pltpu.VMEM(c.shape, BF16) for c in consts],
            dma((8,)), dma((2, 4)), dma((n,)), dma((n,)), dma((n,)), dma((n,)),
            dma((2, 2)), dma((2, 2)), dma((n,)), dma((n,)),
        ],
        compiler_params=pltpu.CompilerParams(collective_id=1, has_side_effects=True, vmem_limit_bytes=60 * 2**20),
    )(envelope, mode_profile, dispersion, kerr_gain.reshape(4, W), *consts)


def solution(mesh):
    placed = (P("mode", None, "tm"), P(), P(None, "mode"), P())
    return jax.shard_map(
        on_device, mesh=mesh, in_specs=placed, out_specs=P("mode", None, "tm"), check_vma=False
    )
```

```python
import functools

import jax
import jax.numpy as jnp
import ml_dtypes
import numpy as np
from jax import lax
from jax.experimental import pallas as pl
from jax.experimental.pallas import tpu as pltpu
from jax.sharding import PartitionSpec as P

FIRST_DIFF = (1.0 / 280, -4.0 / 105, 1.0 / 5, -4.0 / 5, 0.0, 4.0 / 5, -1.0 / 5, 4.0 / 105, -1.0 / 280)
SECOND_DIFF = (-1.0 / 560, 8.0 / 315, -1.0 / 5, 8.0 / 5, -205.0 / 72, 8.0 / 5, -1.0 / 5, 8.0 / 315, -1.0 / 560)
THIRD_DIFF = (7.0 / 240, -3.0 / 10, 169.0 / 120, -61.0 / 30, 0.0, 61.0 / 30, -169.0 / 120, 3.0 / 10, -7.0 / 240)

MESH = pl.DeviceIdType.MESH
F32, BF16 = jnp.float32, jnp.bfloat16
NT = (((1,), (1,)), ((), ()))
TN = (((0,), (0,)), ((), ()))
W = 128


def hi_lo(x):
    hi = x.astype(ml_dtypes.bfloat16)
    lo = (x - hi.astype(np.float64)).astype(ml_dtypes.bfloat16)
    return hi, lo


def constants():
    taps = (np.array(FIRST_DIFF), np.array(SECOND_DIFF) / 2, np.array(THIRD_DIFF) / 6)
    main = np.zeros((W, 3 * W))
    halo = np.zeros((32, 6 * W))
    for which, tap in enumerate(taps):
        for t in range(W):
            for k in range(-4, 5):
                s, col = t + k, which * W + t
                if 0 <= s < W:
                    main[s, col] = tap[k + 4]
                else:
                    row = s + 4 if s < 0 else 16 + s - W
                    halo[row, col] = tap[k + 4]
                    halo[row + 4, 3 * W + col] = tap[k + 4]
    pick = np.zeros((32, 2 * W))
    for j in range(4):
        pick[j, j] = pick[4 + j, W + j] = 1
        pick[16 + j, W - 4 + j] = pick[20 + j, 2 * W - 4 + j] = 1
    return np.concatenate(hi_lo(main), 0), np.concatenate(hi_lo(halo), 0), pick.astype(ml_dtypes.bfloat16)


def dot(a, b, dims=(((1,), (0,)), ((), ()))):
    return lax.dot_general(a, b, dims, preferred_element_type=F32)


def place(y, z, c):
    z = z + (y % 2) * (3 - 2 * z)
    return y * 8 + z * 2 + (c + z) % 2


def device_at(pos):
    y, z = pos // 8, (pos // 2) % 4
    c = (pos % 2 + z) % 2
    z = z + (y % 2) * (3 - 2 * z)
    return y * 8 + z * 2 + c


def kernel(
    peers, count, env_ref, prof_ref, disp_ref, gain_ref, main_ref, halo_ref, pick_ref, out_ref,
    env, prof, proft, own_grid, cubic, field, mid, first, proj, sendbuf, incr, edges, halos, disp, drow, dall, coef, got,
    gain, main, halo, pick, lsem, psem, ssem, rsem, dssem, drsem, hssem, hrsem, bssem, brsem,
):
    me, tm = lax.axis_index("mode"), lax.axis_index("tm")
    slabs = lax.axis_size("tm")
    grid = prof.shape[1]
    parts = psem.shape[1]
    width = grid // parts
    y, z, c = me // 8, (me // 2) % 4, me % 2
    turns = (y, y + 1 - 2 * (y % 2), (y + 2) % 4, 3 - y)

    def to(peer):
        dy, dz, dc = peer
        return turns[dy] * 8 + ((z + dz) % 4) * 2 + (c + dc) % 2

    def back_from(peer):
        return to((peer[0], (4 - peer[1]) % 4, peer[2]))

    def slot(dy, device):
        return dy * 8 + device % 8

    def rows(dy, device):
        return pl.ds(pl.multiple_of(slot(dy, device) * 16, 16), 16)

    here = place(y, z, c)
    right = (device_at((here + 1) % count), (tm + (here + 1) // count) % slabs)
    left = (device_at((here + count - 1) % count), (tm + slabs - (count - here) // count) % slabs)

    barrier = pltpu.get_barrier_semaphore()
    for peer in sorted(peers, key=lambda d: -min(d[1], 4 - d[1])):
        pl.semaphore_signal(barrier, inc=1, device_id=(to(peer), tm), device_id_type=MESH)
    for who in (left, right):
        pl.semaphore_signal(barrier, inc=1, device_id=who, device_id_type=MESH)

    loads = [
        pltpu.make_async_copy(a, b, lsem.at[i])
        for i, (a, b) in enumerate(
            ((env_ref, env), (disp_ref, disp), (gain_ref, gain), (pick_ref, pick), (main_ref, main), (halo_ref, halo))
        )
    ]
    for cp in loads:
        cp.start()

    def prof_in(i, q):
        cols = pl.ds(i * width, width)
        fields = pl.ds(pl.multiple_of(W * turns[q], W), W)
        return pltpu.make_async_copy(prof_ref.at[fields, cols], prof.at[W * q : W * q + W, cols], psem.at[q, i])

    for i in range(parts):
        for q in range(4):
            prof_in(i, q).start()

    loads[0].wait()
    for p in range(count):
        k = place(p // 8, (p // 2) % 4, p % 2)
        block = env[:, :, k * W : (k + 1) * W]
        sendbuf[p, :, 0:W] = block[:, 0, :]
        sendbuf[p, :, W : 2 * W] = block[:, 1, :]
    loads[1].wait()
    drow[...] = jnp.zeros_like(drow)
    drow[0:3, 0:16] = disp[...]
    lines = drow[...]
    drow[0:1, :] = lines[0:1] + pltpu.roll(lines[1:2], 16, 1) + pltpu.roll(lines[2:3], 32, 1)
    dall[me % 8] = drow[0:1, :]

    pl.semaphore_wait(barrier, len(peers) + 2)

    own = pltpu.make_async_copy(sendbuf.at[me], field.at[rows(0, me), :], lsem.at[6])
    own.start()
    sends, dsends = [], []
    for j, peer in enumerate(peers):
        other = to(peer)
        sends.append(pltpu.make_async_remote_copy(
            src_ref=sendbuf.at[other], dst_ref=field.at[rows(peer[0], me), :],
            send_sem=ssem.at[j], recv_sem=rsem.at[j], device_id=(other, tm), device_id_type=MESH))
        sends[-1].start()

    unit = (lax.broadcasted_iota(jnp.int32, (256, 256), 0) == lax.broadcasted_iota(jnp.int32, (256, 256), 1)).astype(BF16)
    for i in range(parts):
        for q in range(4):
            prof_in(i, q).wait()

        def flip(b, _, i=i):
            at = pl.ds(pl.multiple_of(i * width + b * 256, 256), 256)
            for q in (0, 1):
                proft[at, 256 * q : 256 * q + 256] = dot(unit, prof[256 * q : 256 * q + 256, at], NT).astype(BF16)
            return 0

        lax.fori_loop(0, width // 256, flip, 0, unroll=True)

    for j, peer in enumerate(peers):
        dsends.append(pltpu.make_async_remote_copy(
            src_ref=drow.at[0:1], dst_ref=dall.at[slot(peer[0], me)], send_sem=dssem.at[j], recv_sem=drsem.at[j],
            device_id=(to(peer), tm), device_id_type=MESH))
        dsends[-1].start()

    loads[2].wait()
    diagonal = lax.broadcasted_iota(jnp.int32, (W, W), 0) == lax.broadcasted_iota(jnp.int32, (W, W), 1)
    for r in range(4):
        picked = jnp.where(diagonal, gain[pl.ds(turns[r], 1), :] * (256.0 / grid), 0.0)
        coef[3, r * W : (r + 1) * W, :] = jnp.broadcast_to(jnp.sum(picked, 1, keepdims=True), (W, W))

    for cp in loads[3:]:
        cp.wait()

    def grid_field(src, q, at):
        return dot(proft[at, 256 * q : 256 * q + 256], src[256 * q : 256 * q + 256, :])

    step = 2048
    blocks = [slice(b * step, (b + 1) * step) for b in range(grid // step)]

    own.wait()
    for cp, peer in zip(sends, peers):
        if peer[0] < 2:
            cp.wait_recv()

    def coefficients(q):
        lane, sub = (lax.broadcasted_iota(jnp.int32, (16, W), d) for d in (1, 0))
        for i in range(16 * q, 16 * q + 16):
            row = jnp.broadcast_to(dall[i], (16, W))
            for d in range(3):
                column = jnp.sum(jnp.where(lane == sub + 16 * d, row, 0.0), 1, keepdims=True)
                coef[d, 16 * i : 16 * i + 16, :] = jnp.broadcast_to(column, (16, W))

    def form_edges(src, turn, q):
        at = slice(256 * q, 256 * q + 256)
        edges[turn, :, :, at] = dot(pick[...], src[at, :], NT).astype(BF16).reshape(2, 16, 256)

    def send_edges(turn):
        out = []
        for side, who in ((0, left), (1, right)):
            out.append(pltpu.make_async_remote_copy(
                src_ref=edges.at[turn, side], dst_ref=halos.at[turn, 1 - side], send_sem=hssem.at[turn, side],
                recv_sem=hrsem.at[turn, 1 - side], device_id=who, device_id_type=MESH))
            out[-1].start()
        return out

    def cube(g):
        level = g[0][:, :W] ** 2 + g[0][:, W:] ** 2 + g[1][:, :W] ** 2 + g[1][:, W:] ** 2
        level = jnp.concatenate([level, level], 1)
        return [(level * part).astype(BF16) for part in g]

    def interior(src, q):
        at = slice(256 * q, 256 * q + 256)
        values = src[at, :]
        re, im = values[:, :W], values[:, W:]
        d_re = dot(jnp.concatenate([re, re], 1), main[...])
        d_im = dot(jnp.concatenate([im, im], 1), main[...])
        return combined(d_re, d_im, at)

    def column(sender, d):
        row = turns[d]
        return pl.multiple_of(W * (2 * ((sender // 2 + row // 2) % 2) + (sender + row) % 2), W)

    def fringe(turn, q):
        ends = [
            jnp.concatenate([halos[turn, s, :, pl.ds(column(who[0] // 8, d), W)] for d in (2 * q, 2 * q + 1)], 1)
            for s, who in ((0, left), (1, right))
        ]
        side = jnp.concatenate(ends, 0).astype(F32).T.astype(BF16)
        side = dot(jnp.concatenate([side, side], 1), halo[...])
        return combined(side[:, : 3 * W], side[:, 3 * W :], slice(256 * q, 256 * q + 256))

    def combined(d_re, d_im, at):
        walk, spread, skew = (coef[d, at, :] for d in range(3))
        out_re = skew * d_re[:, 2 * W :] - walk * d_re[:, :W] + spread * d_im[:, W : 2 * W]
        out_im = skew * d_im[:, 2 * W :] - walk * d_im[:, :W] - spread * d_re[:, W : 2 * W]
        return jnp.concatenate([out_re, out_im], 1)

    def turned(values, at):
        scale = coef[3, at, :]
        return jnp.concatenate([-scale * values[:, W:], scale * values[:, :W]], 1)

    def arrived(copies, q):
        for cp, peer in zip(copies, peers):
            if peer[0] // 2 == q:
                cp.wait_recv()

    form_edges(field, 0, 0)
    for at in blocks:
        own_grid[at, :] = grid_field(field, 0, at)
    arrived(dsends, 0)
    coefficients(0)
    first[0:256, :] = interior(field, 0)
    arrived(sends, 1)
    form_edges(field, 0, 1)
    hsends = send_edges(0)
    arrived(dsends, 1)
    coefficients(1)
    first[256:512, :] = interior(field, 1)
    for b, at in enumerate(blocks):
        if b == len(blocks) - 1:
            for cp in hsends:
                cp.wait_recv()
            for q in (0, 1):
                first[256 * q : 256 * q + 256, :] += fringe(0, q)
        parts_ = cube([own_grid[at, :], grid_field(field, 1, at)])
        for q in (0, 1):
            part = dot(prof[256 * q : 256 * q + 256, at], parts_[q])
            if b == 0:
                proj[256 * q : 256 * q + 256, :] = part
            else:
                proj[256 * q : 256 * q + 256, :] += part
    for q in (0, 1):
        at = slice(256 * q, 256 * q + 256)
        rate = first[at, :] + turned(proj[at, :], at)
        first[at, :] = rate
        mid[at, :] = (field[at, :].astype(F32) + rate).astype(BF16)
        form_edges(mid, 1, q)
    hsends += send_edges(1)

    for q in (0, 1):
        first[256 * q : 256 * q + 256, :] += interior(mid, q)
    for at in blocks:
        parts_ = cube([grid_field(mid, q, at) for q in (0, 1)])
        for q in (0, 1):
            cubic[q, at, :] = parts_[q]
    returns = {}
    for group in (2, 3, 1, 0):
        at = slice(W * group, W * group + W)
        proj[at, :] = dot(prof[at, :], cubic[group // 2])
        if group == 2:
            for cp in hsends[2:]:
                cp.wait_recv()
            first[256:512, :] += fringe(1, 1)
        if group == 3:
            first[0:256, :] += fringe(1, 0)
        incr[at, :] = (0.5 * (first[at, :] + turned(proj[at, :], at))).astype(BF16)
        for j, peer in enumerate(peers):
            if peer[0] == group:
                other = to(peer)
                returns[j] = pltpu.make_async_remote_copy(
                    src_ref=incr.at[rows(group, other), :], dst_ref=got.at[me], send_sem=bssem.at[j],
                    recv_sem=brsem.at[j], device_id=(other, tm), device_id_type=MESH)
                returns[j].start()
    own = pltpu.make_async_copy(incr.at[rows(0, me), :], got.at[me], lsem.at[7])
    own.start()

    def hand_on(source):
        k = place(source // 8, (source // 2) % 4, source % 2)
        values = got[source].astype(F32)
        pair = jnp.stack([values[:, :W], values[:, W:]], 1)
        at = pl.ds(pl.multiple_of(k * W, W), W)
        out_ref[:, :, at] = env[:, :, at].astype(F32) + pair

    own.wait()
    hand_on(me)
    for j in sorted(range(len(peers)), key=lambda j: ((2, 3, 1, 0).index(peers[j][0]), distance(peers[j]))):
        returns[j].wait_recv()
        hand_on(back_from(peers[j]))
    for cp in [*sends, *dsends, *hsends, *returns.values()]:
        cp.wait_send()


def distance(peer):
    return min(peer[1], 4 - peer[1])


def on_device(envelope, mode_profile, dispersion, kerr_gain):
    count = lax.axis_size("mode")
    peers = [(dy, dz, dc) for dy in range(4) for dz in (2, 1, 3, 0) for dc in range(2) if (dy, dz, dc) != (0, 0, 0)]
    peers.sort(key=lambda d: (d[0] // 2, -min(d[1], 4 - d[1])))
    n = len(peers)
    modes, grid = mode_profile.shape
    consts = [jnp.asarray(c) for c in constants()]
    hbm, vmem = pl.BlockSpec(memory_space=pl.ANY), pl.BlockSpec(memory_space=pltpu.VMEM)
    dma = pltpu.SemaphoreType.DMA
    return pl.pallas_call(
        functools.partial(kernel, peers, count),
        out_shape=pltpu.VMEM(envelope.shape, F32),
        in_specs=[hbm] * 7,
        out_specs=vmem,
        scratch_shapes=[
            pltpu.VMEM(envelope.shape, BF16),
            pltpu.VMEM((modes, grid), BF16),
            pltpu.VMEM((grid, modes), BF16),
            pltpu.VMEM((grid, 2 * W), F32),
            pltpu.VMEM((2, grid, 2 * W), BF16),
            pltpu.VMEM((modes, 2 * W), BF16),
            pltpu.VMEM((modes, 2 * W), BF16),
            pltpu.VMEM((modes, 2 * W), F32),
            pltpu.VMEM((modes, 2 * W), F32),
            pltpu.VMEM((count, 16, 2 * W), BF16),
            pltpu.VMEM((modes, 2 * W), BF16),
            pltpu.VMEM((2, 2, 16, modes), BF16),
            pltpu.VMEM((2, 2, 16, modes), BF16),
            pltpu.VMEM((3, 16), F32),
            pltpu.VMEM((8, W), F32),
            pltpu.VMEM((count, 1, W), F32),
            pltpu.VMEM((4, modes, W), F32),
            pltpu.VMEM((count, 16, 2 * W), BF16),
            pltpu.VMEM((4, W), F32),
            *[pltpu.VMEM(c.shape, BF16) for c in consts],
            dma((8,)), dma((4, 4)), dma((n,)), dma((n,)), dma((n,)), dma((n,)),
            dma((2, 2)), dma((2, 2)), dma((n,)), dma((n,)),
        ],
        compiler_params=pltpu.CompilerParams(collective_id=1, has_side_effects=True, vmem_limit_bytes=60 * 2**20),
    )(envelope, mode_profile, dispersion, kerr_gain.reshape(4, W), *consts)


def solution(mesh):
    placed = (P("mode", None, "tm"), P(), P(None, "mode"), P())
    return jax.shard_map(
        on_device, mesh=mesh, in_specs=placed, out_specs=P("mode", None, "tm"), check_vma=False
    )
```

```python
import functools

import jax
import jax.numpy as jnp
import ml_dtypes
import numpy as np
from jax import lax
from jax.experimental import pallas as pl
from jax.experimental.pallas import tpu as pltpu
from jax.sharding import PartitionSpec as P

FIRST_DIFF = (1.0 / 280, -4.0 / 105, 1.0 / 5, -4.0 / 5, 0.0, 4.0 / 5, -1.0 / 5, 4.0 / 105, -1.0 / 280)
SECOND_DIFF = (-1.0 / 560, 8.0 / 315, -1.0 / 5, 8.0 / 5, -205.0 / 72, 8.0 / 5, -1.0 / 5, 8.0 / 315, -1.0 / 560)
THIRD_DIFF = (7.0 / 240, -3.0 / 10, 169.0 / 120, -61.0 / 30, 0.0, 61.0 / 30, -169.0 / 120, 3.0 / 10, -7.0 / 240)

MESH = pl.DeviceIdType.MESH
F32, BF16 = jnp.float32, jnp.bfloat16
NT = (((1,), (1,)), ((), ()))
TN = (((0,), (0,)), ((), ()))
W = 128


def hi_lo(x):
    hi = x.astype(ml_dtypes.bfloat16)
    lo = (x - hi.astype(np.float64)).astype(ml_dtypes.bfloat16)
    return hi, lo


def constants():
    taps = (np.array(FIRST_DIFF), np.array(SECOND_DIFF) / 2, np.array(THIRD_DIFF) / 6)
    main = np.zeros((W, 3 * W))
    halo = np.zeros((32, 6 * W))
    for which, tap in enumerate(taps):
        for t in range(W):
            for k in range(-4, 5):
                s, col = t + k, which * W + t
                if 0 <= s < W:
                    main[s, col] = tap[k + 4]
                else:
                    row = s + 4 if s < 0 else 16 + s - W
                    halo[row, col] = tap[k + 4]
                    halo[row + 4, 3 * W + col] = tap[k + 4]
    pick = np.zeros((32, 2 * W))
    for j in range(4):
        pick[j, j] = pick[4 + j, W + j] = 1
        pick[16 + j, W - 4 + j] = pick[20 + j, 2 * W - 4 + j] = 1
    return np.concatenate(hi_lo(main), 0), np.concatenate(hi_lo(halo), 0), pick.astype(ml_dtypes.bfloat16)


def dot(a, b, dims=(((1,), (0,)), ((), ()))):
    return lax.dot_general(a, b, dims, preferred_element_type=F32)


def place(y, z, c):
    z = z + (y % 2) * (3 - 2 * z)
    return y * 8 + z * 2 + (c + z) % 2


def device_at(pos):
    y, z = pos // 8, (pos // 2) % 4
    c = (pos % 2 + z) % 2
    z = z + (y % 2) * (3 - 2 * z)
    return y * 8 + z * 2 + c


def kernel(
    peers, count, env_ref, prof_ref, disp_ref, gain_ref, main_ref, halo_ref, pick_ref, out_ref,
    env, prof, proft, own_grid, cubic, field, mid, first, proj, sendbuf, incr, edges, halos, disp, drow, dall, coef, got,
    gain, main, halo, pick, lsem, psem, ssem, rsem, dssem, drsem, hssem, hrsem, bssem, brsem,
):
    me, tm = lax.axis_index("mode"), lax.axis_index("tm")
    slabs = lax.axis_size("tm")
    grid = prof.shape[1]
    parts = psem.shape[1]
    width = grid // parts
    y, z, c = me // 8, (me // 2) % 4, me % 2
    turns = (y, y + 1 - 2 * (y % 2), (y + 2) % 4, 3 - y)

    def to(peer):
        dy, dz, dc = peer
        return turns[dy] * 8 + ((z + dz) % 4) * 2 + (c + dc) % 2

    def back_from(peer):
        return to((peer[0], (4 - peer[1]) % 4, peer[2]))

    def slot(dy, device):
        return dy * 8 + device % 8

    def rows(dy, device):
        return pl.ds(pl.multiple_of(slot(dy, device) * 16, 16), 16)

    here = place(y, z, c)
    right = (device_at((here + 1) % count), (tm + (here + 1) // count) % slabs)
    left = (device_at((here + count - 1) % count), (tm + slabs - (count - here) // count) % slabs)

    barrier = pltpu.get_barrier_semaphore()
    for peer in sorted(peers, key=lambda d: -min(d[1], 4 - d[1])):
        pl.semaphore_signal(barrier, inc=1, device_id=(to(peer), tm), device_id_type=MESH)
    for who in (left, right):
        pl.semaphore_signal(barrier, inc=1, device_id=who, device_id_type=MESH)

    loads = [
        pltpu.make_async_copy(a, b, lsem.at[i])
        for i, (a, b) in enumerate(
            ((env_ref, env), (disp_ref, disp), (gain_ref, gain), (pick_ref, pick), (main_ref, main), (halo_ref, halo))
        )
    ]
    for cp in loads:
        cp.start()

    def prof_in(i, q):
        cols = pl.ds(i * width, width)
        fields = pl.ds(pl.multiple_of(W * turns[q], W), W)
        return pltpu.make_async_copy(prof_ref.at[fields, cols], prof.at[W * q : W * q + W, cols], psem.at[q, i])

    loads[0].wait()
    for p in range(count):
        k = place(p // 8, (p // 2) % 4, p % 2)
        block = env[:, :, k * W : (k + 1) * W]
        sendbuf[p, :, 0:W] = block[:, 0, :]
        sendbuf[p, :, W : 2 * W] = block[:, 1, :]
    loads[1].wait()
    drow[...] = jnp.zeros_like(drow)
    drow[0:3, 0:16] = disp[...]
    lines = drow[...]
    drow[0:1, :] = lines[0:1] + pltpu.roll(lines[1:2], 16, 1) + pltpu.roll(lines[2:3], 32, 1)
    dall[me % 8] = drow[0:1, :]

    pl.semaphore_wait(barrier, len(peers) + 2)

    own = pltpu.make_async_copy(sendbuf.at[me], field.at[rows(0, me), :], lsem.at[6])
    own.start()
    sends, dsends = [], []
    for j, peer in enumerate(peers):
        other = to(peer)
        sends.append(pltpu.make_async_remote_copy(
            src_ref=sendbuf.at[other], dst_ref=field.at[rows(peer[0], me), :],
            send_sem=ssem.at[j], recv_sem=rsem.at[j], device_id=(other, tm), device_id_type=MESH))
        sends[-1].start()

    for j, peer in enumerate(peers):
        dsends.append(pltpu.make_async_remote_copy(
            src_ref=drow.at[0:1], dst_ref=dall.at[slot(peer[0], me)], send_sem=dssem.at[j], recv_sem=drsem.at[j],
            device_id=(to(peer), tm), device_id_type=MESH))
        dsends[-1].start()
    for i in range(parts):
        for q in range(4):
            prof_in(i, q).start()

    unit = (lax.broadcasted_iota(jnp.int32, (256, 256), 0) == lax.broadcasted_iota(jnp.int32, (256, 256), 1)).astype(BF16)
    for i in range(parts):
        for q in range(4):
            prof_in(i, q).wait()

        def flip(b, _, i=i):
            at = pl.ds(pl.multiple_of(i * width + b * 256, 256), 256)
            for q in (0, 1):
                proft[at, 256 * q : 256 * q + 256] = dot(unit, prof[256 * q : 256 * q + 256, at], NT).astype(BF16)
            return 0

        lax.fori_loop(0, width // 256, flip, 0, unroll=True)

    loads[2].wait()
    diagonal = lax.broadcasted_iota(jnp.int32, (W, W), 0) == lax.broadcasted_iota(jnp.int32, (W, W), 1)
    for r in range(4):
        picked = jnp.where(diagonal, gain[pl.ds(turns[r], 1), :] * (256.0 / grid), 0.0)
        coef[3, r * W : (r + 1) * W, :] = jnp.broadcast_to(jnp.sum(picked, 1, keepdims=True), (W, W))

    for cp in loads[3:]:
        cp.wait()

    def grid_field(src, q, at):
        return dot(proft[at, 256 * q : 256 * q + 256], src[256 * q : 256 * q + 256, :])

    step = 2048
    blocks = [slice(b * step, (b + 1) * step) for b in range(grid // step)]

    own.wait()
    for cp, peer in zip(sends, peers):
        if peer[0] < 2:
            cp.wait_recv()

    def coefficients(q):
        lane, sub = (lax.broadcasted_iota(jnp.int32, (16, W), d) for d in (1, 0))
        for i in range(16 * q, 16 * q + 16):
            row = jnp.broadcast_to(dall[i], (16, W))
            for d in range(3):
                column = jnp.sum(jnp.where(lane == sub + 16 * d, row, 0.0), 1, keepdims=True)
                coef[d, 16 * i : 16 * i + 16, :] = jnp.broadcast_to(column, (16, W))

    def form_edges(src, turn, q):
        at = slice(256 * q, 256 * q + 256)
        edges[turn, :, :, at] = dot(pick[...], src[at, :], NT).astype(BF16).reshape(2, 16, 256)

    def send_edges(turn):
        out = []
        for side, who in ((0, left), (1, right)):
            out.append(pltpu.make_async_remote_copy(
                src_ref=edges.at[turn, side], dst_ref=halos.at[turn, 1 - side], send_sem=hssem.at[turn, side],
                recv_sem=hrsem.at[turn, 1 - side], device_id=who, device_id_type=MESH))
            out[-1].start()
        return out

    def cube(g):
        level = g[0][:, :W] ** 2 + g[0][:, W:] ** 2 + g[1][:, :W] ** 2 + g[1][:, W:] ** 2
        level = jnp.concatenate([level, level], 1)
        return [(level * part).astype(BF16) for part in g]

    def interior(src, q):
        at = slice(256 * q, 256 * q + 256)
        values = src[at, :]
        re, im = values[:, :W], values[:, W:]
        d_re = dot(jnp.concatenate([re, re], 1), main[...])
        d_im = dot(jnp.concatenate([im, im], 1), main[...])
        return combined(d_re, d_im, at)

    def column(sender, d):
        row = turns[d]
        return pl.multiple_of(W * (2 * ((sender // 2 + row // 2) % 2) + (sender + row) % 2), W)

    def fringe(turn, q):
        ends = [
            jnp.concatenate([halos[turn, s, :, pl.ds(column(who[0] // 8, d), W)] for d in (2 * q, 2 * q + 1)], 1)
            for s, who in ((0, left), (1, right))
        ]
        side = jnp.concatenate(ends, 0).astype(F32).T.astype(BF16)
        side = dot(jnp.concatenate([side, side], 1), halo[...])
        return combined(side[:, : 3 * W], side[:, 3 * W :], slice(256 * q, 256 * q + 256))

    def combined(d_re, d_im, at):
        walk, spread, skew = (coef[d, at, :] for d in range(3))
        out_re = skew * d_re[:, 2 * W :] - walk * d_re[:, :W] + spread * d_im[:, W : 2 * W]
        out_im = skew * d_im[:, 2 * W :] - walk * d_im[:, :W] - spread * d_re[:, W : 2 * W]
        return jnp.concatenate([out_re, out_im], 1)

    def turned(values, at):
        scale = coef[3, at, :]
        return jnp.concatenate([-scale * values[:, W:], scale * values[:, :W]], 1)

    def arrived(copies, q):
        for cp, peer in zip(copies, peers):
            if peer[0] // 2 == q:
                cp.wait_recv()

    form_edges(field, 0, 0)
    for at in blocks:
        own_grid[at, :] = grid_field(field, 0, at)
    arrived(dsends, 0)
    coefficients(0)
    first[0:256, :] = interior(field, 0)
    arrived(sends, 1)
    form_edges(field, 0, 1)
    hsends = send_edges(0)
    arrived(dsends, 1)
    coefficients(1)
    first[256:512, :] = interior(field, 1)
    for b, at in enumerate(blocks):
        parts_ = cube([own_grid[at, :], grid_field(field, 1, at)])
        for q in (0, 1):
            part = dot(prof[256 * q : 256 * q + 256, at], parts_[q])
            if b == 0:
                proj[256 * q : 256 * q + 256, :] = part
            else:
                proj[256 * q : 256 * q + 256, :] += part
    for cp in hsends:
        cp.wait_recv()
    for q in (0, 1):
        at = slice(256 * q, 256 * q + 256)
        rate = first[at, :] + fringe(0, q) + turned(proj[at, :], at)
        first[at, :] = rate
        mid[at, :] = (field[at, :].astype(F32) + rate).astype(BF16)
        form_edges(mid, 1, q)
    hsends += send_edges(1)

    for q in (0, 1):
        first[256 * q : 256 * q + 256, :] += interior(mid, q)
    for at in blocks:
        parts_ = cube([grid_field(mid, q, at) for q in (0, 1)])
        for q in (0, 1):
            cubic[q, at, :] = parts_[q]
    returns = {}
    for group in (2, 3, 1, 0):
        at = slice(W * group, W * group + W)
        proj[at, :] = dot(prof[at, :], cubic[group // 2])
        if group == 2:
            for cp in hsends[2:]:
                cp.wait_recv()
            first[256:512, :] += fringe(1, 1)
        if group == 3:
            first[0:256, :] += fringe(1, 0)
        incr[at, :] = (0.5 * (first[at, :] + turned(proj[at, :], at))).astype(BF16)
        for j, peer in enumerate(peers):
            if peer[0] == group:
                other = to(peer)
                returns[j] = pltpu.make_async_remote_copy(
                    src_ref=incr.at[rows(group, other), :], dst_ref=got.at[me], send_sem=bssem.at[j],
                    recv_sem=brsem.at[j], device_id=(other, tm), device_id_type=MESH)
                returns[j].start()
    own = pltpu.make_async_copy(incr.at[rows(0, me), :], got.at[me], lsem.at[7])
    own.start()

    def hand_on(source):
        k = place(source // 8, (source // 2) % 4, source % 2)
        values = got[source].astype(F32)
        pair = jnp.stack([values[:, :W], values[:, W:]], 1)
        at = pl.ds(pl.multiple_of(k * W, W), W)
        out_ref[:, :, at] = env[:, :, at].astype(F32) + pair

    own.wait()
    hand_on(me)
    for j in sorted(range(len(peers)), key=lambda j: ((2, 3, 1, 0).index(peers[j][0]), distance(peers[j]))):
        returns[j].wait_recv()
        hand_on(back_from(peers[j]))
    for cp in [*sends, *dsends, *hsends, *returns.values()]:
        cp.wait_send()


def distance(peer):
    return min(peer[1], 4 - peer[1])


def on_device(envelope, mode_profile, dispersion, kerr_gain):
    count = lax.axis_size("mode")
    peers = [(dy, dz, dc) for dy in range(4) for dz in (2, 1, 3, 0) for dc in range(2) if (dy, dz, dc) != (0, 0, 0)]
    peers.sort(key=lambda d: (d[0] // 2, -min(d[1], 4 - d[1])))
    n = len(peers)
    modes, grid = mode_profile.shape
    consts = [jnp.asarray(c) for c in constants()]
    hbm, vmem = pl.BlockSpec(memory_space=pl.ANY), pl.BlockSpec(memory_space=pltpu.VMEM)
    dma = pltpu.SemaphoreType.DMA
    return pl.pallas_call(
        functools.partial(kernel, peers, count),
        out_shape=pltpu.VMEM(envelope.shape, F32),
        in_specs=[hbm] * 7,
        out_specs=vmem,
        scratch_shapes=[
            pltpu.VMEM(envelope.shape, BF16),
            pltpu.VMEM((modes, grid), BF16),
            pltpu.VMEM((grid, modes), BF16),
            pltpu.VMEM((grid, 2 * W), F32),
            pltpu.VMEM((2, grid, 2 * W), BF16),
            pltpu.VMEM((modes, 2 * W), BF16),
            pltpu.VMEM((modes, 2 * W), BF16),
            pltpu.VMEM((modes, 2 * W), F32),
            pltpu.VMEM((modes, 2 * W), F32),
            pltpu.VMEM((count, 16, 2 * W), BF16),
            pltpu.VMEM((modes, 2 * W), BF16),
            pltpu.VMEM((2, 2, 16, modes), BF16),
            pltpu.VMEM((2, 2, 16, modes), BF16),
            pltpu.VMEM((3, 16), F32),
            pltpu.VMEM((8, W), F32),
            pltpu.VMEM((count, 1, W), F32),
            pltpu.VMEM((4, modes, W), F32),
            pltpu.VMEM((count, 16, 2 * W), BF16),
            pltpu.VMEM((4, W), F32),
            *[pltpu.VMEM(c.shape, BF16) for c in consts],
            dma((8,)), dma((4, 4)), dma((n,)), dma((n,)), dma((n,)), dma((n,)),
            dma((2, 2)), dma((2, 2)), dma((n,)), dma((n,)),
        ],
        compiler_params=pltpu.CompilerParams(collective_id=1, has_side_effects=True, vmem_limit_bytes=60 * 2**20),
    )(envelope, mode_profile, dispersion, kerr_gain.reshape(4, W), *consts)


def solution(mesh):
    placed = (P("mode", None, "tm"), P(), P(None, "mode"), P())
    return jax.shard_map(
        on_device, mesh=mesh, in_specs=placed, out_specs=P("mode", None, "tm"), check_vma=False
    )
```

```python
import functools

import jax
import jax.numpy as jnp
import ml_dtypes
import numpy as np
from jax import lax
from jax.experimental import pallas as pl
from jax.experimental.pallas import tpu as pltpu
from jax.sharding import PartitionSpec as P

FIRST_DIFF = (1.0 / 280, -4.0 / 105, 1.0 / 5, -4.0 / 5, 0.0, 4.0 / 5, -1.0 / 5, 4.0 / 105, -1.0 / 280)
SECOND_DIFF = (-1.0 / 560, 8.0 / 315, -1.0 / 5, 8.0 / 5, -205.0 / 72, 8.0 / 5, -1.0 / 5, 8.0 / 315, -1.0 / 560)
THIRD_DIFF = (7.0 / 240, -3.0 / 10, 169.0 / 120, -61.0 / 30, 0.0, 61.0 / 30, -169.0 / 120, 3.0 / 10, -7.0 / 240)

MESH = pl.DeviceIdType.MESH
F32, BF16 = jnp.float32, jnp.bfloat16
NT = (((1,), (1,)), ((), ()))
TN = (((0,), (0,)), ((), ()))
W = 128


def hi_lo(x):
    hi = x.astype(ml_dtypes.bfloat16)
    lo = (x - hi.astype(np.float64)).astype(ml_dtypes.bfloat16)
    return hi, lo


def constants():
    taps = (np.array(FIRST_DIFF), np.array(SECOND_DIFF) / 2, np.array(THIRD_DIFF) / 6)
    main = np.zeros((W, 3 * W))
    halo = np.zeros((32, 6 * W))
    for which, tap in enumerate(taps):
        for t in range(W):
            for k in range(-4, 5):
                s, col = t + k, which * W + t
                if 0 <= s < W:
                    main[s, col] = tap[k + 4]
                else:
                    row = s + 4 if s < 0 else 16 + s - W
                    halo[row, col] = tap[k + 4]
                    halo[row + 4, 3 * W + col] = tap[k + 4]
    pick = np.zeros((32, 2 * W))
    for j in range(4):
        pick[j, j] = pick[4 + j, W + j] = 1
        pick[16 + j, W - 4 + j] = pick[20 + j, 2 * W - 4 + j] = 1
    return np.concatenate(hi_lo(main), 0), np.concatenate(hi_lo(halo), 0), pick.astype(ml_dtypes.bfloat16)


def dot(a, b, dims=(((1,), (0,)), ((), ()))):
    return lax.dot_general(a, b, dims, preferred_element_type=F32)


def place(y, z, c):
    z = z + (y % 2) * (3 - 2 * z)
    return y * 8 + z * 2 + (c + z) % 2


def device_at(pos):
    y, z = pos // 8, (pos // 2) % 4
    c = (pos % 2 + z) % 2
    z = z + (y % 2) * (3 - 2 * z)
    return y * 8 + z * 2 + c


def kernel(
    peers, count, env_ref, prof_ref, disp_ref, gain_ref, main_ref, halo_ref, pick_ref, out_ref,
    env, prof, proft, own_grid, cubic, field, mid, first, proj, sendbuf, incr, edges, halos, disp, drow, dall, coef, got,
    gain, main, halo, pick, lsem, psem, ssem, rsem, dssem, drsem, hssem, hrsem, bssem, brsem,
):
    me, tm = lax.axis_index("mode"), lax.axis_index("tm")
    slabs = lax.axis_size("tm")
    grid = prof.shape[1]
    parts = psem.shape[1]
    width = grid // parts
    y, z, c = me // 8, (me // 2) % 4, me % 2
    turns = (y, y + 1 - 2 * (y % 2), (y + 2) % 4, 3 - y)

    def to(peer):
        dy, dz, dc = peer
        return turns[dy] * 8 + ((z + dz) % 4) * 2 + (c + dc) % 2

    def back_from(peer):
        return to((peer[0], (4 - peer[1]) % 4, peer[2]))

    def slot(dy, device):
        return dy * 8 + device % 8

    def rows(dy, device):
        return pl.ds(pl.multiple_of(slot(dy, device) * 16, 16), 16)

    here = place(y, z, c)
    right = (device_at((here + 1) % count), (tm + (here + 1) // count) % slabs)
    left = (device_at((here + count - 1) % count), (tm + slabs - (count - here) // count) % slabs)

    barrier = pltpu.get_barrier_semaphore()
    for peer in sorted(peers, key=lambda d: -min(d[1], 4 - d[1])):
        pl.semaphore_signal(barrier, inc=1, device_id=(to(peer), tm), device_id_type=MESH)
    for who in (left, right):
        pl.semaphore_signal(barrier, inc=1, device_id=who, device_id_type=MESH)

    loads = [
        pltpu.make_async_copy(a, b, lsem.at[i])
        for i, (a, b) in enumerate(
            ((env_ref, env), (disp_ref, disp), (gain_ref, gain), (pick_ref, pick), (main_ref, main), (halo_ref, halo))
        )
    ]
    for cp in loads:
        cp.start()

    def prof_in(i, q):
        cols = pl.ds(i * width, width)
        fields = pl.ds(pl.multiple_of(W * turns[q], W), W)
        return pltpu.make_async_copy(prof_ref.at[fields, cols], prof.at[W * q : W * q + W, cols], psem.at[q, i])

    loads[0].wait()
    for p in range(count):
        k = place(p // 8, (p // 2) % 4, p % 2)
        block = env[:, :, k * W : (k + 1) * W]
        sendbuf[p, :, 0:W] = block[:, 0, :]
        sendbuf[p, :, W : 2 * W] = block[:, 1, :]
    loads[1].wait()
    drow[...] = jnp.zeros_like(drow)
    drow[0:3, 0:16] = disp[...]
    lines = drow[...]
    drow[0:1, :] = lines[0:1] + pltpu.roll(lines[1:2], 16, 1) + pltpu.roll(lines[2:3], 32, 1)
    dall[me % 8] = drow[0:1, :]

    pl.semaphore_wait(barrier, len(peers) + 2)

    own = pltpu.make_async_copy(sendbuf.at[me], field.at[rows(0, me), :], lsem.at[6])
    own.start()
    sends, dsends = [], []
    for j, peer in enumerate(peers):
        other = to(peer)
        sends.append(pltpu.make_async_remote_copy(
            src_ref=sendbuf.at[other], dst_ref=field.at[rows(peer[0], me), :],
            send_sem=ssem.at[j], recv_sem=rsem.at[j], device_id=(other, tm), device_id_type=MESH))
        sends[-1].start()

    for j, peer in enumerate(peers):
        dsends.append(pltpu.make_async_remote_copy(
            src_ref=drow.at[0:1], dst_ref=dall.at[slot(peer[0], me)], send_sem=dssem.at[j], recv_sem=drsem.at[j],
            device_id=(to(peer), tm), device_id_type=MESH))
        dsends[-1].start()
    for i in range(parts):
        for q in range(4):
            prof_in(i, q).start()

    unit = (lax.broadcasted_iota(jnp.int32, (256, 256), 0) == lax.broadcasted_iota(jnp.int32, (256, 256), 1)).astype(BF16)
    for i in range(parts):
        for q in range(4):
            prof_in(i, q).wait()

        def flip(b, _, i=i):
            at = pl.ds(pl.multiple_of(i * width + b * 256, 256), 256)
            for q in (0, 1):
                proft[at, 256 * q : 256 * q + 256] = dot(unit, prof[256 * q : 256 * q + 256, at], NT).astype(BF16)
            return 0

        lax.fori_loop(0, width // 256, flip, 0, unroll=True)

    loads[2].wait()
    diagonal = lax.broadcasted_iota(jnp.int32, (W, W), 0) == lax.broadcasted_iota(jnp.int32, (W, W), 1)
    for r in range(4):
        picked = jnp.where(diagonal, gain[pl.ds(turns[r], 1), :] * (256.0 / grid), 0.0)
        coef[3, r * W : (r + 1) * W, :] = jnp.broadcast_to(jnp.sum(picked, 1, keepdims=True), (W, W))

    for cp in loads[3:]:
        cp.wait()

    def grid_field(src, q, at):
        return dot(proft[at, 256 * q : 256 * q + 256], src[256 * q : 256 * q + 256, :])

    step = 2048
    blocks = [slice(b * step, (b + 1) * step) for b in range(grid // step)]

    own.wait()
    for cp, peer in zip(sends, peers):
        if peer[0] < 2:
            cp.wait_recv()

    def coefficients(q):
        lane, sub = (lax.broadcasted_iota(jnp.int32, (16, W), d) for d in (1, 0))
        for i in range(16 * q, 16 * q + 16):
            row = jnp.broadcast_to(dall[i], (16, W))
            for d in range(3):
                column = jnp.sum(jnp.where(lane == sub + 16 * d, row, 0.0), 1, keepdims=True)
                coef[d, 16 * i : 16 * i + 16, :] = jnp.broadcast_to(column, (16, W))

    def form_edges(src, turn, q):
        at = slice(256 * q, 256 * q + 256)
        edges[turn, :, :, at] = dot(pick[...], src[at, :], NT).astype(BF16).reshape(2, 16, 256)

    def send_edges(turn):
        out = []
        for side, who in ((0, left), (1, right)):
            out.append(pltpu.make_async_remote_copy(
                src_ref=edges.at[turn, side], dst_ref=halos.at[turn, 1 - side], send_sem=hssem.at[turn, side],
                recv_sem=hrsem.at[turn, 1 - side], device_id=who, device_id_type=MESH))
            out[-1].start()
        return out

    def cube(g):
        level = g[0][:, :W] ** 2 + g[0][:, W:] ** 2 + g[1][:, :W] ** 2 + g[1][:, W:] ** 2
        level = jnp.concatenate([level, level], 1)
        return [(level * part).astype(BF16) for part in g]

    def interior(src, q):
        at = slice(256 * q, 256 * q + 256)
        values = src[at, :]
        re, im = values[:, :W], values[:, W:]
        d_re = dot(jnp.concatenate([re, re], 1), main[...])
        d_im = dot(jnp.concatenate([im, im], 1), main[...])
        return combined(d_re, d_im, at)

    def column(sender, d):
        row = turns[d]
        return pl.multiple_of(W * (2 * ((sender // 2 + row // 2) % 2) + (sender + row) % 2), W)

    def fringe(turn, q):
        ends = [
            jnp.concatenate([halos[turn, s, :, pl.ds(column(who[0] // 8, d), W)] for d in (2 * q, 2 * q + 1)], 1)
            for s, who in ((0, left), (1, right))
        ]
        side = jnp.concatenate(ends, 0).astype(F32).T.astype(BF16)
        side = dot(jnp.concatenate([side, side], 1), halo[...])
        return combined(side[:, : 3 * W], side[:, 3 * W :], slice(256 * q, 256 * q + 256))

    def combined(d_re, d_im, at):
        walk, spread, skew = (coef[d, at, :] for d in range(3))
        out_re = skew * d_re[:, 2 * W :] - walk * d_re[:, :W] + spread * d_im[:, W : 2 * W]
        out_im = skew * d_im[:, 2 * W :] - walk * d_im[:, :W] - spread * d_re[:, W : 2 * W]
        return jnp.concatenate([out_re, out_im], 1)

    def turned(values, at):
        scale = coef[3, at, :]
        return jnp.concatenate([-scale * values[:, W:], scale * values[:, :W]], 1)

    def arrived(copies, q):
        for cp, peer in zip(copies, peers):
            if peer[0] // 2 == q:
                cp.wait_recv()

    form_edges(field, 0, 0)
    for at in blocks:
        own_grid[at, :] = grid_field(field, 0, at)
    arrived(dsends, 0)
    coefficients(0)
    first[0:256, :] = interior(field, 0)
    arrived(sends, 1)
    form_edges(field, 0, 1)
    hsends = send_edges(0)
    arrived(dsends, 1)
    coefficients(1)
    first[256:512, :] = interior(field, 1)
    for b, at in enumerate(blocks):
        parts_ = cube([own_grid[at, :], grid_field(field, 1, at)])
        for q in (0, 1):
            part = dot(prof[256 * q : 256 * q + 256, at], parts_[q])
            if b == 0:
                proj[256 * q : 256 * q + 256, :] = part
            else:
                proj[256 * q : 256 * q + 256, :] += part
    for cp in hsends:
        cp.wait_recv()
    for q in (0, 1):
        at = slice(256 * q, 256 * q + 256)
        rate = first[at, :] + fringe(0, q) + turned(proj[at, :], at)
        first[at, :] = rate
        mid[at, :] = (field[at, :].astype(F32) + rate).astype(BF16)
        form_edges(mid, 1, q)
    hsends += send_edges(1)

    for q in (0, 1):
        first[256 * q : 256 * q + 256, :] += interior(mid, q)
    for at in blocks:
        parts_ = cube([grid_field(mid, q, at) for q in (0, 1)])
        for q in (0, 1):
            cubic[q, at, :] = parts_[q]
    returns = {}
    for group in (2, 3, 1, 0):
        at = slice(W * group, W * group + W)
        proj[at, :] = dot(prof[at, :], cubic[group // 2])
        if group == 2:
            for cp in hsends[2:]:
                cp.wait_recv()
            first[256:512, :] += fringe(1, 1)
        if group == 3:
            first[0:256, :] += fringe(1, 0)
        incr[at, :] = (0.5 * (first[at, :] + turned(proj[at, :], at))).astype(BF16)
        for j, peer in enumerate(peers):
            if peer[0] == group:
                other = to(peer)
                returns[j] = pltpu.make_async_remote_copy(
                    src_ref=incr.at[rows(group, other), :], dst_ref=got.at[me], send_sem=bssem.at[j],
                    recv_sem=brsem.at[j], device_id=(other, tm), device_id_type=MESH)
                returns[j].start()
    own = pltpu.make_async_copy(incr.at[rows(0, me), :], got.at[me], lsem.at[7])
    own.start()

    def hand_on(source):
        k = place(source // 8, (source // 2) % 4, source % 2)
        values = got[source].astype(F32)
        pair = jnp.stack([values[:, :W], values[:, W:]], 1)
        at = pl.ds(pl.multiple_of(k * W, W), W)
        out_ref[:, :, at] = env[:, :, at].astype(F32) + pair

    own.wait()
    hand_on(me)
    for j in sorted(range(len(peers)), key=lambda j: ((2, 3, 1, 0).index(peers[j][0]), distance(peers[j]))):
        returns[j].wait_recv()
        hand_on(back_from(peers[j]))
    for cp in [*sends, *dsends, *hsends, *returns.values()]:
        cp.wait_send()


def distance(peer):
    return min(peer[1], 4 - peer[1])


def on_device(envelope, mode_profile, dispersion, kerr_gain):
    count = lax.axis_size("mode")
    peers = [(dy, dz, dc) for dy in range(4) for dz in (2, 1, 3, 0) for dc in range(2) if (dy, dz, dc) != (0, 0, 0)]
    rank = {(0, 2): 0, (0, 1): 1, (1, 2): 2, (0, 0): 3, (1, 1): 4, (1, 0): 5}
    peers.sort(key=lambda d: rank[d[0] // 2, min(d[1], 4 - d[1])])
    n = len(peers)
    modes, grid = mode_profile.shape
    consts = [jnp.asarray(c) for c in constants()]
    hbm, vmem = pl.BlockSpec(memory_space=pl.ANY), pl.BlockSpec(memory_space=pltpu.VMEM)
    dma = pltpu.SemaphoreType.DMA
    return pl.pallas_call(
        functools.partial(kernel, peers, count),
        out_shape=pltpu.VMEM(envelope.shape, F32),
        in_specs=[hbm] * 7,
        out_specs=vmem,
        scratch_shapes=[
            pltpu.VMEM(envelope.shape, BF16),
            pltpu.VMEM((modes, grid), BF16),
            pltpu.VMEM((grid, modes), BF16),
            pltpu.VMEM((grid, 2 * W), F32),
            pltpu.VMEM((2, grid, 2 * W), BF16),
            pltpu.VMEM((modes, 2 * W), BF16),
            pltpu.VMEM((modes, 2 * W), BF16),
            pltpu.VMEM((modes, 2 * W), F32),
            pltpu.VMEM((modes, 2 * W), F32),
            pltpu.VMEM((count, 16, 2 * W), BF16),
            pltpu.VMEM((modes, 2 * W), BF16),
            pltpu.VMEM((2, 2, 16, modes), BF16),
            pltpu.VMEM((2, 2, 16, modes), BF16),
            pltpu.VMEM((3, 16), F32),
            pltpu.VMEM((8, W), F32),
            pltpu.VMEM((count, 1, W), F32),
            pltpu.VMEM((4, modes, W), F32),
            pltpu.VMEM((count, 16, 2 * W), BF16),
            pltpu.VMEM((4, W), F32),
            *[pltpu.VMEM(c.shape, BF16) for c in consts],
            dma((8,)), dma((4, 4)), dma((n,)), dma((n,)), dma((n,)), dma((n,)),
            dma((2, 2)), dma((2, 2)), dma((n,)), dma((n,)),
        ],
        compiler_params=pltpu.CompilerParams(collective_id=1, has_side_effects=True, vmem_limit_bytes=60 * 2**20),
    )(envelope, mode_profile, dispersion, kerr_gain.reshape(4, W), *consts)


def solution(mesh):
    placed = (P("mode", None, "tm"), P(), P(None, "mode"), P())
    return jax.shard_map(
        on_device, mesh=mesh, in_specs=placed, out_specs=P("mode", None, "tm"), check_vma=False
    )
```
